128 devices in a mesh: outer: 8 (over y, core), inner: 16 (over x, z).
Axes of the slice: x: 4, y: 4, z: 4, core: 2. Of those that a mesh axis runs over, the one named last changes fastest.
Arguments:
- points: float32 [262144, 64], P(('outer', 'inner')), may hold values from -2.5 to 2.5
- charges: float32 [262144, 128], P(('outer', 'inner')), may hold values from -0.4 to 0.4
- interp: float32 [262144, 256], P(('outer', 'inner')), may hold values from -0.25 to 0.25
- order: int32 [262144], P(('outer', 'inner')), may hold values from 0 to 262143, as said below
- near: int32 [512, 8], replicated, may hold values from 0 to 511, as said below
- far: int32 [512, 8], replicated, may hold values from 0 to 511, as said below
- skel: int32 [512, 256], P(('outer', 'inner')), may hold values from 0 to 511, as said below
Outputs:
- potential: float32 [262144, 128], P(('outer', 'inner'))
The draws below stay inside these ranges and needn't reach their ends.
Inputs may be any that keep to these rules, and one draw needn't show every extreme that they name: `order`: A permutation; tree position p lies on device p // 2048 in the rows' layout, and each device's rows hold exactly 16 positions of every device. `near`: row g names leaf g first, then 8 - 1 distinct leaves on other devices with the same outer index (leaf h lies on device h // 4); the entries of one device's leaves name at most 2 leaves on any one other device, counting repeats, and some pair of devices reaches 2. `far`: row g names 8 distinct leaves on devices with the same inner index as leaf g and another outer index. `skel`: each row holds distinct values.
All inputs are finite; a program needn't handle non-finite values.
Results may differ from the reference program's by a relative error of at most 0.000082.
Values sent between devices are 32-bit elements; how exact they have to be, the bound alone decides.
A program may use at most 128 MiB of HBM per device.

```python
import jax
import jax.numpy as jnp
from jax import lax

DIM = 64
RHS = 128
LEAF = 512
SKEL = 256
NEAR = 8
FARS = 8
LEAF_DEV = 4
POINTS = 262144
N_OUTER = 8
N_INNER = 16


def order_table(key):
    device_total = N_OUTER * N_INNER
    row_total = LEAF_DEV * LEAF
    per_device = row_total // device_total
    halves = jax.random.split(jax.random.fold_in(key, 11), 2)
    dest_perm = jax.vmap(lambda sub: jax.random.permutation(sub, row_total))(jax.random.split(halves[0], device_total))
    src_perm = jax.vmap(lambda sub: jax.random.permutation(sub, row_total))(jax.random.split(halves[1], device_total))
    tree_pos = jnp.arange(device_total, dtype=jnp.int32)[None, :, None] * row_total + jnp.transpose(dest_perm.reshape(device_total, device_total, per_device), (1, 0, 2)).astype(jnp.int32)
    orig_pos = jnp.arange(device_total, dtype=jnp.int32)[:, None, None] * row_total + src_perm.reshape(device_total, device_total, per_device).astype(jnp.int32)
    table = jnp.zeros((device_total * row_total,), jnp.int32)
    return table.at[orig_pos.reshape(-1)].set(tree_pos.reshape(-1))


def draw_order(key, part):
    return order_table(key)


def draw_points(key, part):
    placed = order_table(key)
    leaf_total = N_OUTER * N_INNER * LEAF_DEV
    centers = jnp.clip(0.25 * jax.random.normal(jax.random.fold_in(key, 12), (leaf_total, DIM), jnp.float32), -1.0, 1.0)
    noise = jnp.clip(0.3 * jax.random.normal(jax.random.fold_in(key, 13), (leaf_total * LEAF, DIM), jnp.float32), -1.5, 1.5)
    tree_ordered_points = jnp.repeat(centers, LEAF, axis=0) + noise
    return tree_ordered_points[placed]


def draw_near(key, part):
    device_total = N_OUTER * N_INNER
    remote = NEAR - 1
    entries = LEAF_DEV * remote
    peer_total = N_INNER - 1
    capacity = (entries + N_INNER - 2) // (N_INNER - 1)

    def one_device(dev_key, device):
        first_key, second_key = jax.random.split(dev_key)
        local_pick = jax.vmap(lambda sub: jax.random.permutation(sub, LEAF_DEV)[:capacity])(jax.random.split(first_key, peer_total))
        chosen = jax.random.permutation(second_key, peer_total * capacity)[:entries]
        peer_slot = chosen // capacity
        local_leaf = local_pick.reshape(-1)[chosen]
        outer_pos = device // N_INNER
        inner_pos = device % N_INNER
        peer_inner = (inner_pos + 1 + peer_slot) % N_INNER
        listed = (outer_pos * N_INNER + peer_inner) * LEAF_DEV + local_leaf
        own_leaf = device * LEAF_DEV + jnp.arange(LEAF_DEV, dtype=jnp.int32)
        return jnp.concatenate([own_leaf[:, None], listed.reshape(LEAF_DEV, remote).astype(jnp.int32)], axis=1)
    tables = jax.vmap(one_device)(jax.random.split(jax.random.fold_in(key, 21), device_total), jnp.arange(device_total, dtype=jnp.int32))
    return tables.reshape(device_total * LEAF_DEV, NEAR).astype(jnp.int32)


def draw_far(key, part):
    leaf_total = N_OUTER * N_INNER * LEAF_DEV
    candidates = (N_OUTER - 1) * LEAF_DEV

    def one_leaf(leaf_key, leaf_id):
        picked = jax.random.permutation(leaf_key, candidates)[:FARS]
        device = leaf_id // LEAF_DEV
        outer_pos = device // N_INNER
        inner_pos = device % N_INNER
        other_outer = (outer_pos + 1 + picked // LEAF_DEV) % N_OUTER
        return ((other_outer * N_INNER + inner_pos) * LEAF_DEV + picked % LEAF_DEV).astype(jnp.int32)
    return jax.vmap(one_leaf)(jax.random.split(jax.random.fold_in(key, 31), leaf_total), jnp.arange(leaf_total, dtype=jnp.int32))


def draw_skel(key, part):
    leaf_total = N_OUTER * N_INNER * LEAF_DEV
    picks = jax.vmap(lambda sub: jax.random.permutation(sub, LEAF)[:SKEL])(jax.random.split(jax.random.fold_in(key, 41), leaf_total))
    return picks.astype(jnp.int32)


def levels(own_key, extent, cuts, least, largest):
    level, own = 1.0, jax.random.fold_in(own_key, 6)
    for dim, parts in cuts:
        draws = jnp.exp(jax.random.uniform(jax.random.fold_in(own, dim), (parts,), jnp.float32, least / len(cuts), largest / len(cuts)))
        level = level * jnp.repeat(draws, extent[dim] // parts).reshape([-1 if axis == dim else 1 for axis in range(len(extent))])
    return level


def bell_draw(stream_key, dims, deviation, limit, shards=(), held_as=jnp.bfloat16):
    values = deviation * jax.random.normal(stream_key, dims, jnp.float32)
    if shards:
        values = values * levels(stream_key, dims, shards, -0.22, 0.18)
    return jnp.clip(values, -limit, limit).astype(held_as)


def setup_inputs(seed: int = 0) -> dict:
    splits = jax.random.split(jax.random.key(seed), 8)
    return {
        "points": draw_points(jax.random.fold_in(splits[7], 71), 0),
        "charges": bell_draw(splits[1], (POINTS, RHS), 0.05, 0.4, ((0, 128),), jnp.float32),
        "interp": bell_draw(splits[2], (POINTS, SKEL), LEAF ** -0.5, 0.25, ((0, 128),), jnp.float32),
        "order": draw_order(jax.random.fold_in(splits[7], 71), 0),
        "near": draw_near(jax.random.fold_in(splits[7], 71), 0),
        "far": draw_far(jax.random.fold_in(splits[7], 71), 0),
        "skel": draw_skel(jax.random.fold_in(splits[7], 71), 0),
    }


def apply_tile(target, source, source_chg):
    cross = jnp.dot(target, source.T, precision=lax.Precision.HIGHEST, preferred_element_type=jnp.float32)
    dist_sq = jnp.sum(target * target, axis=1)[:, None] + jnp.sum(source * source, axis=1)[None, :] - 2.0 * cross
    kernel = jnp.exp(-dist_sq * (4.0 / target.shape[1]))
    return jnp.dot(kernel, source_chg, precision=lax.Precision.HIGHEST, preferred_element_type=jnp.float32)


def listed_sum(target, sources, source_chg):
    return jnp.sum(jax.vmap(lambda source, charge: apply_tile(target, source, charge))(sources, source_chg), axis=0)


def reference(points, charges, interp, order, near, far, skel):
    tree_ordered_points = jnp.zeros_like(points).at[order].set(points)
    tree_chg = jnp.zeros_like(charges).at[order].set(charges)
    leaf_total = near.shape[0]
    leaf_size = tree_ordered_points.shape[0] // leaf_total
    leaf_pts = tree_ordered_points.reshape(leaf_total, leaf_size, -1)
    leaf_charge_block = tree_chg.reshape(leaf_total, leaf_size, -1)
    leaf_interpolant = interp.reshape(leaf_total, leaf_size, -1)
    skel_pts = jnp.take_along_axis(leaf_pts, skel[:, :, None], axis=1)
    skeleton_charge = jnp.einsum("euq,eub->eqb", leaf_interpolant, leaf_charge_block, precision=lax.Precision.HIGHEST)

    def one_leaf(index):
        near_part = listed_sum(leaf_pts[index], leaf_pts[near[index]], leaf_charge_block[near[index]])
        skeleton_potential = listed_sum(skel_pts[index], skel_pts[far[index]], skeleton_charge[far[index]])
        far_field_part = jnp.dot(leaf_interpolant[index], skeleton_potential, precision=lax.Precision.HIGHEST, preferred_element_type=jnp.float32)
        return near_part + far_field_part

    tree_pot = lax.map(one_leaf, jnp.arange(leaf_total, dtype=jnp.int32))
    return tree_pot.reshape(tree_ordered_points.shape[0], -1)[order]
```

```python
import functools
import math

import jax
import jax.numpy as jnp
from jax import lax
from jax.experimental import pallas as pl
from jax.experimental.pallas import tpu as pltpu
from jax.sharding import PartitionSpec as P

F32, BF16, I32 = jnp.float32, jnp.bfloat16, jnp.int32
MESH = pl.DeviceIdType.MESH
VMEM_LIMIT = 60 * 1024 * 1024

ROWS = 2048
DEVS = 128
LEAF = 512
HALF = 256
DIM = 64
RHS = 128
BLK = HALF + 128
SCALE = math.log2(math.e) * 4.0 / DIM


def vspec():
    return pl.BlockSpec(memory_space=pltpu.VMEM)


def sspec():
    return pl.BlockSpec(memory_space=pltpu.SMEM)


def dot(a, b, contract=((1,), (0,))):
    return lax.dot_general(a, b, (contract, ((), ())), preferred_element_type=F32)


def hi_lo(v):
    hi = v.astype(BF16)
    return hi, (v - hi.astype(F32)).astype(BF16)


def dot3(a, b, contract=((1,), (0,))):
    ah, al = hi_lo(a)
    bh, bl = hi_lo(b)
    return dot(ah, bh, contract) + dot(ah, bl, contract) + dot(al, bh, contract)


def three(v):
    hi = v.astype(BF16).astype(F32)
    rest = v - hi
    mid = rest.astype(BF16).astype(F32)
    return hi, mid, rest - mid


def rank_kernel(order_ref, rank_ref):
    sub = lax.broadcasted_iota(I32, (128, 128), 0)
    lane = lax.broadcasted_iota(I32, (128, 128), 1)
    before = (sub < lane).astype(F32).astype(BF16)
    ones = jnp.ones((128, 128), BF16)
    base = jnp.zeros((128, 128), F32)
    for r in range(ROWS // 128):
        owner = order_ref[r : r + 1, :] // ROWS
        hit = (sub == owner).astype(F32)
        hit16 = hit.astype(BF16)
        seen = dot(hit16, before) + base
        base = base + dot(hit16, ones)
        count = jnp.sum(hit * seen, axis=0, keepdims=True)
        rank_ref[r : r + 1, :] = owner * 16 + count.astype(I32)


def rank_rows(order):
    return pl.pallas_call(
        rank_kernel,
        out_shape=jax.ShapeDtypeStruct((ROWS // 128, 128), I32),
        in_specs=[vspec()],
        out_specs=vspec(),
    )(order.reshape(ROWS // 128, 128))


def send_kernel(rank_ref, order_ref, pts_ref, chg_ref, sent_ref, wide):
    lane = lax.broadcasted_iota(I32, (128, 128), 1)
    for r in range(ROWS // 128):
        rows = pl.ds(r * 128, 128)
        wide[rows, 0:DIM] = pts_ref[rows, :]
        pos = (order_ref[r : r + 1, :] % ROWS).astype(F32)
        column = jnp.transpose(jnp.broadcast_to(pos, (128, 128)))
        wide[rows, DIM:128] = column[:, 0:DIM]

    def body(b, carry):
        for u in range(16):
            n = b * 16 + u
            to = rank_ref[n]
            dev, row = to // 16, to % 16
            sent_ref[dev, pl.ds(row, 1), :] = chg_ref[pl.ds(n, 1), :]
            sent_ref[dev, pl.ds(row + 16, 1), :] = wide[pl.ds(n, 1), :]
        return carry

    lax.fori_loop(0, ROWS // 16, body, 0)


def pack_rows(rank, order, points, charges):
    return pl.pallas_call(
        send_kernel,
        out_shape=jax.ShapeDtypeStruct((DEVS, 32, 128), F32),
        in_specs=[sspec(), vspec(), vspec(), vspec()],
        out_specs=vspec(),
        scratch_shapes=[pltpu.VMEM((ROWS, 128), F32)],
        compiler_params=pltpu.CompilerParams(vmem_limit_bytes=VMEM_LIMIT),
    )(rank, order.reshape(ROWS // 128, 128), points, charges)


def target_operand(x):
    n = x.shape[0]
    hi, lo = hi_lo(x * (2.0 * SCALE))
    norm = jnp.sum(x * x, axis=1, keepdims=True) * (-SCALE)
    n0, n1, n2 = three(norm)
    lane = lax.broadcasted_iota(I32, (n, DIM), 1)
    tail = jnp.where(
        lane == 0, n0, jnp.where(lane == 1, n1, jnp.where(lane == 2, n2, jnp.where(lane < 6, 1.0, 0.0)))
    )
    return jnp.concatenate([hi, hi, lo, tail.astype(BF16)], axis=1)


def place_kernel(pos_ref, skel_ref, got_ref, interp_ref, blk_ref, fblk_ref, tgt_ref, stgt_ref, pts, chg, sk):
    def place(b, carry):
        for u in range(16):
            at = pos_ref[b * 16 + u]
            chg[pl.ds(at, 1), :] = got_ref[b, u : u + 1, :]
            pts[pl.ds(at, 1), :] = got_ref[b, 16 + u : 17 + u, :]
        return carry

    lax.fori_loop(0, DEVS, place, 0)

    def leaf(g, carry):
        def pick(b, inner):
            for u in range(16):
                q = b * 16 + u
                sk[pl.ds(q, 1), :] = pts[pl.ds(g * LEAF + skel_ref[g, q], 1), :]
            return inner

        lax.fori_loop(0, 16, pick, 0)
        for h in range(2):
            rows = pl.ds(pl.multiple_of(g * LEAF + h * HALF, HALF), HALF)
            blk_ref[h, g, 0:HALF, :] = chg[rows, :]
            x = pts[rows, :]
            xt = jnp.transpose(x)
            blk_ref[h, g, HALF : HALF + 64, :] = xt[0:64, 0:128]
            blk_ref[h, g, HALF + 64 : BLK, :] = xt[0:64, 128:256]
            tgt_ref[g, h * HALF : (h + 1) * HALF, :] = target_operand(x[:, 0:DIM])
        s = sk[...]
        st = jnp.transpose(s)
        fblk_ref[g, HALF : HALF + 64, :] = st[0:64, 0:128]
        fblk_ref[g, HALF + 64 : BLK, :] = st[0:64, 128:256]
        stgt_ref[g] = target_operand(s[:, 0:DIM])
        rows = pl.ds(pl.multiple_of(g * LEAF, LEAF), LEAF)
        fblk_ref[g, 0:HALF, :] = dot3(interp_ref[rows, :], chg[rows, :], ((0,), (0,)))
        return carry

    lax.fori_loop(0, 4, leaf, 0)


def place_rows(pos, skel, got, interp):
    return pl.pallas_call(
        place_kernel,
        out_shape=[
            jax.ShapeDtypeStruct((2, 4, BLK, 128), F32),
            jax.ShapeDtypeStruct((4, BLK, 128), F32),
            jax.ShapeDtypeStruct((4, LEAF, 256), BF16),
            jax.ShapeDtypeStruct((4, HALF, 256), BF16),
        ],
        in_specs=[sspec(), sspec(), vspec(), vspec()],
        out_specs=[vspec()] * 4,
        scratch_shapes=[
            pltpu.VMEM((ROWS, 128), F32),
            pltpu.VMEM((ROWS, 128), F32),
            pltpu.VMEM((HALF, 128), F32),
        ],
        compiler_params=pltpu.CompilerParams(vmem_limit_bytes=VMEM_LIMIT),
    )(pos, skel, got, interp)


def source_operand(block, scale):
    xt = jnp.concatenate([block[HALF : HALF + 64, :], block[HALF + 64 : BLK, :]], axis=1)
    hi, lo = hi_lo(xt)
    norm = jnp.sum(xt * xt, axis=0, keepdims=True) * (-SCALE)
    n0, n1, n2 = three(norm)
    row = lax.broadcasted_iota(I32, (16, HALF), 0)
    tail = jnp.where(
        row < 3, 1.0, jnp.where(row == 3, n0, jnp.where(row == 4, n1, jnp.where(row == 5, n2, 0.0)))
    )
    right = jnp.concatenate([hi, lo, hi, tail.astype(BF16), jnp.zeros((48, HALF), BF16)], axis=0)
    chg = block[0:HALF, :]
    if scale is not None:
        chg = chg * scale
    ch, cl = hi_lo(chg)
    return right, jnp.concatenate([ch, cl], axis=1), ch


def tile(target, operand):
    right, both, ch = operand
    g = jnp.exp2(dot(target, right))
    gh, gl = hi_lo(g)
    wide = dot(gh, both)
    return wide[:, 0:128] + wide[:, 128:256] + dot(gl, ch)


STEP = 128


def exchange_kernel(
    code, near_at, far_at, blk, fblk, tgt, stgt, interp, pot,
    p1a1, p1a2, p1a3, p1b1, p1b2, p1b3, sb, p2, p3, fb, ob,
    s1, r1, s2, r2, s3, r3, sf, rf,
):
    o, i = lax.axis_index("outer"), lax.axis_index("inner")
    y, c, x, z = o // 2, o % 2, i // 4, i % 4
    p1 = ((None, p1a1, p1a2, p1a3), (None, p1b1, p1b2, p1b3))

    def at_inner(dx, dz):
        return ((x + dx + 4) % 4) * 4 + (z + dz + 4) % 4

    def off(h, d1, d2):
        return at_inner(d1, d2) if h == 0 else at_inner(d2, d1)

    def first(h, d):
        return (o, off(h, d, 0))

    def second(h, d):
        return (o, off(h, 0, d))

    def along_y(d):
        return (((y + d + 4) % 4) * 2 + c, i)

    sibling = (y * 2 + 1 - c, i)

    barrier = pltpu.get_barrier_semaphore()
    peers = [first(0, 1), first(0, -1), second(0, 1), second(0, -1), along_y(1), along_y(-1), sibling]
    for peer in peers:
        pl.semaphore_signal(barrier, inc=1, device_id=peer, device_id_type=MESH)
    pl.semaphore_wait(barrier, len(peers))

    def copy(src, dst, send, recv, to):
        return pltpu.make_async_remote_copy(
            src_ref=src, dst_ref=dst, send_sem=send, recv_sem=recv, device_id=to, device_id_type=MESH
        )

    def own_first(h, k):
        return copy(blk.at[h], p1[h][1 if k == 0 else 3], s1.at[h, k], r1.at[h, k], first(h, 1 if k == 0 else -1))

    def onward(h, k):
        part = pl.ds(2 * k, 2)
        src = p1[h][1 if k == 0 else 3].at[part]
        return copy(src, p1[h][2].at[part], s1.at[h, 2 + k], r1.at[h, 2 + k], first(h, 1 if k == 0 else -1))

    def slots(h, d, k):
        return copy(sb.at[h, d, k], p2.at[h, d, k], s2.at[h, d, k], r2.at[h, d, k], second(h, 1 if k == 0 else -1))

    def relay(h, d, k):
        return copy(p2.at[h, d, k, 2], p3.at[h, d, k], s3.at[h, d, k], r3.at[h, d, k], second(h, 1 if k == 0 else -1))

    def fbuf(dy, dc, lo=0, n=4):
        return fb.at[pl.ds((dy * 2 + dc - 1) * 4 + lo, n)]

    far_copies = {
        "up": copy(fblk, fbuf(1, 0), sf.at[0], rf.at[0], along_y(1)),
        "down": copy(fblk, fbuf(3, 0), sf.at[1], rf.at[1], along_y(-1)),
        "own": copy(fblk, fbuf(0, 1), sf.at[2], rf.at[2], sibling),
        "up2": copy(fbuf(1, 0, 0, 2), fbuf(2, 0, 0, 2), sf.at[3], rf.at[3], along_y(1)),
        "down2": copy(fbuf(3, 0, 2, 2), fbuf(2, 0, 2, 2), sf.at[4], rf.at[4], along_y(-1)),
        "side1": copy(fbuf(1, 0), fbuf(1, 1), sf.at[5], rf.at[5], sibling),
        "side3": copy(fbuf(3, 0), fbuf(3, 1), sf.at[6], rf.at[6], sibling),
        "side2": copy(fbuf(2, 0), fbuf(2, 1), sf.at[7], rf.at[7], sibling),
    }

    def leaf_code(dest, src, j):
        return code[(dest * 16 + src) * 2 + j]

    def fill(h, d):
        src = off(h, -d, 0)
        for k in range(2):
            for slot in range(3):
                dest = off(h, 0, (1 if k == 0 else -1) if slot < 2 else 2)
                leaf = leaf_code(dest, src, slot if slot < 2 else k) % 4
                if d == 0:
                    sb[h, d, k, slot] = blk[h, leaf]
                else:
                    sb[h, d, k, slot] = p1[h][d][leaf]
            slots(h, d, k).start()

    def add_tile(block, g, scale, at, n=LEAF):
        operand = source_operand(block, scale)
        for r in range(0, n, STEP):
            rows = pl.ds(r, STEP)
            ob[at, rows, :] += tile(tgt[g, rows, :], operand)

    def slot_tiles(h, d, e, which):
        dx, dz = (d, e) if h == 0 else (e, d)
        src = at_inner(-dx, -dz)
        for j, load in which:
            v = leaf_code(i, src, j)
            add_tile(load(v % 4), (v // 4) % 4, (v // 16).astype(F32), (dx * 4 + dz) * 2 + j)

    own_first(0, 0).start()
    own_first(0, 1).start()
    own_first(1, 0).start()
    own_first(1, 1).start()
    far_copies["up"].start()
    far_copies["down"].start()
    far_copies["own"].start()
    fill(0, 0)
    fill(1, 0)

    def zero(t, carry):
        ob[t] = jnp.zeros((LEAF, 128), F32)
        return carry

    lax.fori_loop(0, 32, zero, 0)

    def own(t, carry):
        g, h = t // 2, t % 2
        add_tile(blk[h, g], g, None, 0)
        rows = pl.ds(pl.multiple_of(g * LEAF, LEAF), LEAF)

        @pl.when(h == 1)
        def _():
            pot[rows, :] = ob[0]
            ob[0] = jnp.zeros((LEAF, 128), F32)

        return carry

    lax.fori_loop(0, 8, own, 0)

    for k in range(2):
        for h in range(2):
            own_first(h, k).wait_recv()
            onward(h, k).start()
            fill(h, 1 if k == 0 else 3)
    for name, more in (("up", ("up2", "side1")), ("down", ("down2", "side3")), ("own", ())):
        far_copies[name].wait_recv()
        for m in more:
            far_copies[m].start()

    def first_tiles(d):
        for h in range(2):
            slot_tiles(h, d, 0, [(j, lambda leaf, b=p1[h][d]: b[leaf]) for j in range(2)])

    first_tiles(1)
    far_copies["up2"].wait_recv()
    far_copies["down2"].wait_recv()
    far_copies["side2"].start()
    for h in range(2):
        onward(h, 0).wait_recv()
        onward(h, 1).wait_recv()
        fill(h, 2)
    first_tiles(3)

    def arrive(d):
        for h in range(2):
            for k in range(2):
                slots(h, d, k).wait_recv()
                relay(h, d, k).start()

    def second_tiles(d):
        for h in range(2):
            for k in range(2):
                slot_tiles(h, d, 1 if k == 0 else 3, [(j, lambda leaf, k=k, j=j: p2[h, d, k, j]) for j in range(2)])

    arrive(0)
    first_tiles(2)
    second_tiles(0)
    for name in ("side1", "side3", "side2"):
        far_copies[name].wait_recv()

    def far_leaf(g, carry):
        def one(k, q):
            operand = source_operand(fb[far_at[g * 8 + k]], None)
            return q + tile(stgt[g], operand)

        q = lax.fori_loop(0, 8, one, jnp.zeros((HALF, 128), F32))
        rows = pl.ds(pl.multiple_of(g * LEAF, LEAF), LEAF)
        pot[rows, :] += dot3(interp[rows, :], q)
        return carry

    lax.fori_loop(0, 4, far_leaf, 0)

    def relay_tiles(d):
        for h in range(2):
            for k in range(2):
                relay(h, d, k).wait_recv()
            slot_tiles(h, d, 2, [(j, lambda leaf, j=j: p3[h, d, j]) for j in range(2)])

    arrive(1)
    second_tiles(1)
    arrive(3)
    second_tiles(3)
    relay_tiles(0)
    arrive(2)
    second_tiles(2)
    relay_tiles(1)
    relay_tiles(3)
    relay_tiles(2)

    def finish(g, carry):
        rows = pl.ds(pl.multiple_of(g * LEAF, LEAF), LEAF)
        total = pot[rows, :]
        for k in range(7):
            total = total + ob[near_at[g * 7 + k]]
        pot[rows, :] = total
        return carry

    lax.fori_loop(0, 4, finish, 0)

    for h in range(2):
        for k in range(2):
            own_first(h, k).wait_send()
            onward(h, k).wait_send()
            for d in range(4):
                slots(h, d, k).wait_send()
                relay(h, d, k).wait_send()
    for one in far_copies.values():
        one.wait_send()


def exchange(code, near_at, far_at, blk, fblk, tgt, stgt, interp):
    dma = pltpu.SemaphoreType.DMA
    return pl.pallas_call(
        exchange_kernel,
        out_shape=jax.ShapeDtypeStruct((ROWS, RHS), F32),
        in_specs=[sspec()] * 3 + [vspec()] * 5,
        out_specs=vspec(),
        scratch_shapes=[pltpu.VMEM((4, BLK, 128), F32)] * 6
        + [
            pltpu.VMEM((2, 4, 2, 3, BLK, 128), F32),
            pltpu.VMEM((2, 4, 2, 3, BLK, 128), F32),
            pltpu.VMEM((2, 4, 2, BLK, 128), F32),
            pltpu.VMEM((28, BLK, 128), F32),
            pltpu.VMEM((32, LEAF, 128), F32),
            dma((2, 4)),
            dma((2, 4)),
            dma((2, 4, 2)),
            dma((2, 4, 2)),
            dma((2, 4, 2)),
            dma((2, 4, 2)),
            dma((8,)),
            dma((8,)),
        ],
        compiler_params=pltpu.CompilerParams(
            vmem_limit_bytes=VMEM_LIMIT, collective_id=0, has_side_effects=True
        ),
    )(code, near_at, far_at, blk, fblk, tgt, stgt, interp)


def gather_kernel(idx_ref, src_ref, dst_ref):
    def body(b, carry):
        for u in range(16):
            n = b * 16 + u
            dst_ref[pl.ds(n, 1), :] = src_ref[pl.ds(idx_ref[n], 1), :]
        return carry

    lax.fori_loop(0, ROWS // 16, body, 0)


def gather_rows(idx, src):
    return pl.pallas_call(
        gather_kernel,
        out_shape=jax.ShapeDtypeStruct((ROWS, RHS), F32),
        in_specs=[sspec(), vspec()],
        out_specs=vspec(),
        compiler_params=pltpu.CompilerParams(vmem_limit_bytes=VMEM_LIMIT),
    )(idx, src)


def tables(near, far):
    o, i = lax.axis_index("outer"), lax.axis_index("inner")
    y, c, x, z = o // 2, o % 2, i // 4, i % 4
    rows = lax.dynamic_slice_in_dim(near, o * 64, 64, 0)
    entry = rows[:, 1:].reshape(16, 28)
    src, leaf = (entry // 4) % 16, entry % 4
    target = jnp.arange(28, dtype=I32) // 7
    earlier = jnp.arange(28)[:, None] > jnp.arange(28)[None, :]
    nth = jnp.sum(((src[:, :, None] == src[:, None, :]) & earlier[None]).astype(I32), axis=2)
    mark = 16 + 4 * target[None, :] + leaf
    place = src * 2 + nth
    hit = place[:, :, None] == jnp.arange(32, dtype=I32)[None, None, :]
    code = jnp.sum(jnp.where(hit, mark[:, :, None], 0), axis=1).reshape(512)
    mine = lax.dynamic_slice_in_dim(src, i, 1, 0)[0]
    mine_nth = lax.dynamic_slice_in_dim(nth, i, 1, 0)[0]
    near_at = (((x - mine // 4) % 4) * 4 + (z - mine % 4) % 4) * 2 + mine_nth
    f = lax.dynamic_slice_in_dim(far, (o * 16 + i) * 4, 4, 0).reshape(32)
    fo = f // 64
    far_at = (((y - fo // 2) % 4) * 2 + (c + fo) % 2 - 1) * 4 + f % 4
    return code.astype(I32), near_at.astype(I32), far_at.astype(I32)


def shards(points, charges, interp, order, near, far, skel):
    axes = ("outer", "inner")
    code, near_at, far_at = tables(near, far)
    rank = rank_rows(order).reshape(ROWS)
    sent = pack_rows(rank, order, points, charges)
    got = lax.all_to_all(sent, axes, split_axis=0, concat_axis=0, tiled=True)
    pos = got[:, 16:32, DIM].astype(I32).reshape(ROWS)
    blk, fblk, tgt, stgt = place_rows(pos, skel, got, interp)
    pot = exchange(code, near_at, far_at, blk, fblk, tgt, stgt, interp)
    back = gather_rows(pos, pot).reshape(DEVS, 16, RHS)
    back = lax.all_to_all(back, axes, split_axis=0, concat_axis=0, tiled=True)
    return gather_rows(rank, back.reshape(ROWS, RHS))


def solution(mesh):
    rows = P(("outer", "inner"), None)
    return jax.shard_map(
        shards,
        mesh=mesh,
        in_specs=(rows, rows, rows, P(("outer", "inner")), P(), P(), rows),
        out_specs=rows,
        check_vma=False,
    )
```

```python
import functools
import math

import jax
import jax.numpy as jnp
from jax import lax
from jax.experimental import pallas as pl
from jax.experimental.pallas import tpu as pltpu
from jax.sharding import PartitionSpec as P

F32, BF16, I32 = jnp.float32, jnp.bfloat16, jnp.int32
MESH = pl.DeviceIdType.MESH
VMEM_LIMIT = 60 * 1024 * 1024

ROWS = 2048
DEVS = 128
LEAF = 512
HALF = 256
DIM = 64
RHS = 128
BLK = HALF + 128
SCALE = math.log2(math.e) * 4.0 / DIM


def vspec():
    return pl.BlockSpec(memory_space=pltpu.VMEM)


def sspec():
    return pl.BlockSpec(memory_space=pltpu.SMEM)


def dot(a, b, contract=((1,), (0,))):
    return lax.dot_general(a, b, (contract, ((), ())), preferred_element_type=F32)


def hi_lo(v):
    hi = v.astype(BF16)
    return hi, (v - hi.astype(F32)).astype(BF16)


def dot3(a, b, contract=((1,), (0,))):
    ah, al = hi_lo(a)
    bh, bl = hi_lo(b)
    return dot(ah, bh, contract) + dot(ah, bl, contract) + dot(al, bh, contract)


def three(v):
    hi = v.astype(BF16).astype(F32)
    rest = v - hi
    mid = rest.astype(BF16).astype(F32)
    return hi, mid, rest - mid


def rank_kernel(order_ref, rank_ref, slot_ref):
    sub = lax.broadcasted_iota(I32, (128, 128), 0)
    lane = lax.broadcasted_iota(I32, (128, 128), 1)
    before = (sub < lane).astype(F32).astype(BF16)
    ones = jnp.ones((128, 128), BF16)
    base = jnp.zeros((128, 128), F32)
    for r in range(ROWS // 128):
        owner = order_ref[r : r + 1, :] >> 11
        hit = (sub == owner).astype(F32)
        hit16 = hit.astype(BF16)
        seen = dot(hit16, before) + base
        base = base + dot(hit16, ones)
        count = jnp.sum(hit * seen, axis=0, keepdims=True)
        nth = count.astype(I32)
        rank_ref[r : r + 1, :] = owner * 16 + nth
        slot_ref[r : r + 1, :] = owner * 32 + nth


def rank_rows(order):
    return pl.pallas_call(
        rank_kernel,
        out_shape=[jax.ShapeDtypeStruct((ROWS // 128, 128), I32)] * 2,
        in_specs=[vspec()],
        out_specs=[vspec()] * 2,
    )(order.reshape(ROWS // 128, 128))


def send_kernel(slot_ref, order_ref, pts_ref, chg_ref, sent_ref, wide):
    for r in range(ROWS // 128):
        pos = (order_ref[r : r + 1, :] & (ROWS - 1)).astype(F32)
        both = jnp.concatenate([pts_ref[:, r * 128 : (r + 1) * 128], jnp.broadcast_to(pos, (DIM, 128))], axis=0)
        wide[r * 128 : (r + 1) * 128, :] = jnp.transpose(both)

    def body(b, carry):
        first = pl.multiple_of(b * 16, 16)
        to = [slot_ref[first + u] for u in range(16)]
        chg = [chg_ref[pl.ds(first + u, 1), :] for u in range(16)]
        pts = [wide[pl.ds(first + u, 1), :] for u in range(16)]
        for u in range(16):
            sent_ref[pl.ds(to[u], 1), :] = chg[u]
            sent_ref[pl.ds(to[u] + 16, 1), :] = pts[u]
        return carry

    lax.fori_loop(0, ROWS // 16, body, 0)


def pack_rows(slot, order, points, charges):
    return pl.pallas_call(
        send_kernel,
        out_shape=jax.ShapeDtypeStruct((DEVS * 32, 128), F32),
        in_specs=[sspec(), vspec(), vspec(), vspec()],
        out_specs=vspec(),
        scratch_shapes=[pltpu.VMEM((ROWS, 128), F32)],
        compiler_params=pltpu.CompilerParams(vmem_limit_bytes=VMEM_LIMIT),
    )(slot, order.reshape(ROWS // 128, 128), points.T, charges)


def target_operand(x):
    n = x.shape[0]
    hi, lo = hi_lo(x * (2.0 * SCALE))
    norm = jnp.sum(x * x, axis=1, keepdims=True) * (-SCALE)
    n0, n1, n2 = three(norm)
    lane = lax.broadcasted_iota(I32, (n, DIM), 1)
    tail = jnp.where(
        lane == 0, n0, jnp.where(lane == 1, n1, jnp.where(lane == 2, n2, jnp.where(lane < 6, 1.0, 0.0)))
    )
    return jnp.concatenate([hi, hi, lo, tail.astype(BF16)], axis=1)


def place_kernel(pos_ref, skel_ref, got_ref, interp_ref, blk_ref, fblk_ref, tgt_ref, stgt_ref, pts, chg, sk):
    def place(b, carry):
        at = [pos_ref[b * 16 + u] for u in range(16)]
        c = [got_ref[b, u : u + 1, :] for u in range(16)]
        p = [got_ref[b, 16 + u : 17 + u, :] for u in range(16)]
        for u in range(16):
            chg[pl.ds(at[u], 1), :] = c[u]
            pts[pl.ds(at[u], 1), :] = p[u]
        return carry

    lax.fori_loop(0, DEVS, place, 0)

    def leaf(g, carry):
        def pick(b, inner):
            rows = [pts[pl.ds(g * LEAF + skel_ref[g, b * 16 + u], 1), :] for u in range(16)]
            for u in range(16):
                sk[pl.ds(b * 16 + u, 1), :] = rows[u]
            return inner

        lax.fori_loop(0, 16, pick, 0)
        for h in range(2):
            rows = pl.ds(pl.multiple_of(g * LEAF + h * HALF, HALF), HALF)
            blk_ref[h, g, 0:HALF, :] = chg[rows, :]
            x = pts[rows, :]
            xt = jnp.transpose(x)
            blk_ref[h, g, HALF : HALF + 64, :] = xt[0:64, 0:128]
            blk_ref[h, g, HALF + 64 : BLK, :] = xt[0:64, 128:256]
            tgt_ref[g, h * HALF : (h + 1) * HALF, :] = target_operand(x[:, 0:DIM])
        s = sk[...]
        st = jnp.transpose(s)
        fblk_ref[g, HALF : HALF + 64, :] = st[0:64, 0:128]
        fblk_ref[g, HALF + 64 : BLK, :] = st[0:64, 128:256]
        stgt_ref[g] = target_operand(s[:, 0:DIM])
        rows = pl.ds(pl.multiple_of(g * LEAF, LEAF), LEAF)
        fblk_ref[g, 0:HALF, :] = dot3(interp_ref[rows, :], chg[rows, :], ((0,), (0,)))
        return carry

    lax.fori_loop(0, 4, leaf, 0)


def place_rows(pos, skel, got, interp):
    return pl.pallas_call(
        place_kernel,
        out_shape=[
            jax.ShapeDtypeStruct((2, 4, BLK, 128), F32),
            jax.ShapeDtypeStruct((4, BLK, 128), F32),
            jax.ShapeDtypeStruct((4, LEAF, 256), BF16),
            jax.ShapeDtypeStruct((4, HALF, 256), BF16),
        ],
        in_specs=[sspec(), sspec(), vspec(), vspec()],
        out_specs=[vspec()] * 4,
        scratch_shapes=[
            pltpu.VMEM((ROWS, 128), F32),
            pltpu.VMEM((ROWS, 128), F32),
            pltpu.VMEM((HALF, 128), F32),
        ],
        compiler_params=pltpu.CompilerParams(vmem_limit_bytes=VMEM_LIMIT),
    )(pos, skel, got, interp)


def source_operand(block, scale):
    xt = jnp.concatenate([block[HALF : HALF + 64, :], block[HALF + 64 : BLK, :]], axis=1)
    hi, lo = hi_lo(xt)
    norm = jnp.sum(xt * xt, axis=0, keepdims=True) * (-SCALE)
    n0, n1, n2 = three(norm)
    row = lax.broadcasted_iota(I32, (16, HALF), 0)
    tail = jnp.where(
        row < 3, 1.0, jnp.where(row == 3, n0, jnp.where(row == 4, n1, jnp.where(row == 5, n2, 0.0)))
    )
    right = jnp.concatenate([hi, lo, hi, tail.astype(BF16), jnp.zeros((48, HALF), BF16)], axis=0)
    chg = block[0:HALF, :]
    if scale is not None:
        chg = chg * scale
    ch, cl = hi_lo(chg)
    return right, jnp.concatenate([ch, cl], axis=1)


def tile(target, operand):
    right, both = operand
    n = target.shape[0]
    g = jnp.exp2(dot(target, right))
    gh, gl = hi_lo(g)
    wide = dot(jnp.concatenate([gh, gl], axis=0), both)
    return wide[:n, 0:128] + (wide[:n, 128:256] + wide[n:, 0:128])


def exchange_kernel(
    code, near_at, far_at, blk, fblk, tgt, stgt, interp, pot,
    p1a1, p1a2, p1a3, p1b1, p1b2, p1b3, sb, p2, p3, fb, ob,
    s1, r1, s2, r2, s3, r3, s4, r4, sf, rf,
):
    o, i = lax.axis_index("outer"), lax.axis_index("inner")
    y, c, x, z = o // 2, o % 2, i // 4, i % 4
    p1 = ((None, p1a1, p1a2, p1a3), (None, p1b1, p1b2, p1b3))

    def at_inner(dx, dz):
        return ((x + dx + 4) % 4) * 4 + (z + dz + 4) % 4

    def off(h, d1, d2):
        return at_inner(d1, d2) if h == 0 else at_inner(d2, d1)

    def first(h, d):
        return (o, off(h, d, 0))

    def second(h, d):
        return (o, off(h, 0, d))

    def along_y(d):
        return (((y + d + 4) % 4) * 2 + c, i)

    sibling = (y * 2 + 1 - c, i)

    barrier = pltpu.get_barrier_semaphore()
    peers = [first(0, 1), first(0, -1), second(0, 1), second(0, -1), along_y(1), along_y(-1), sibling]
    for peer in peers:
        pl.semaphore_signal(barrier, inc=1, device_id=peer, device_id_type=MESH)
    pl.semaphore_wait(barrier, len(peers))

    def copy(src, dst, send, recv, to):
        return pltpu.make_async_remote_copy(
            src_ref=src, dst_ref=dst, send_sem=send, recv_sem=recv, device_id=to, device_id_type=MESH
        )

    def own_first(h, k):
        return copy(blk.at[h], p1[h][1 if k == 0 else 3], s1.at[h, k], r1.at[h, k], first(h, 1 if k == 0 else -1))

    def onward(h, k):
        part = pl.ds(2 * k, 2)
        src = p1[h][1 if k == 0 else 3].at[part]
        return copy(src, p1[h][2].at[part], s1.at[h, 2 + k], r1.at[h, 2 + k], first(h, 1 if k == 0 else -1))

    def slots(h, d, k):
        two = pl.ds(0, 2)
        to = second(h, 1 if k == 0 else -1)
        return copy(sb.at[h, d, k, two], p2.at[h, d, k, two], s2.at[h, d, k], r2.at[h, d, k], to)

    def ahead(h, d, k):
        to = second(h, 1 if k == 0 else -1)
        return copy(sb.at[h, d, k, 2], p2.at[h, d, k, 2], s4.at[h, d, k], r4.at[h, d, k], to)

    def relay(h, d, k):
        return copy(p2.at[h, d, k, 2], p3.at[h, d, k], s3.at[h, d, k], r3.at[h, d, k], second(h, 1 if k == 0 else -1))

    def fbuf(dy, dc, lo=0, n=4):
        return fb.at[pl.ds((dy * 2 + dc - 1) * 4 + lo, n)]

    far_copies = {
        "up": copy(fblk, fbuf(1, 0), sf.at[0], rf.at[0], along_y(1)),
        "down": copy(fblk, fbuf(3, 0), sf.at[1], rf.at[1], along_y(-1)),
        "own": copy(fblk, fbuf(0, 1), sf.at[2], rf.at[2], sibling),
        "up2": copy(fbuf(1, 0, 0, 2), fbuf(2, 0, 0, 2), sf.at[3], rf.at[3], along_y(1)),
        "down2": copy(fbuf(3, 0, 2, 2), fbuf(2, 0, 2, 2), sf.at[4], rf.at[4], along_y(-1)),
        "side1": copy(fbuf(1, 0), fbuf(1, 1), sf.at[5], rf.at[5], sibling),
        "side3": copy(fbuf(3, 0), fbuf(3, 1), sf.at[6], rf.at[6], sibling),
        "side2": copy(fbuf(2, 0), fbuf(2, 1), sf.at[7], rf.at[7], sibling),
    }

    def leaf_code(dest, src, j):
        return code[(dest * 16 + src) * 2 + j]

    def fill(h, d):
        src = off(h, -d, 0)
        for k in range(2):
            for slot in (2, 0, 1):
                dest = off(h, 0, (1 if k == 0 else -1) if slot < 2 else 2)
                leaf = leaf_code(dest, src, slot if slot < 2 else k) % 4
                if d == 0:
                    sb[h, d, k, slot] = blk[h, leaf]
                else:
                    sb[h, d, k, slot] = p1[h][d][leaf]
                if slot == 2:
                    ahead(h, d, k).start()
            slots(h, d, k).start()

    def add_tile(block, g, scale, at):
        ob[at] += tile(tgt[g], source_operand(block, scale))

    def slot_tiles(h, d, e, which):
        dx, dz = (d, e) if h == 0 else (e, d)
        src = at_inner(-dx, -dz)
        for j, load in which:
            v = leaf_code(i, src, j)
            add_tile(load(v % 4), (v // 4) % 4, (v // 16).astype(F32), (dx * 4 + dz) * 2 + j)

    own_first(0, 0).start()
    own_first(0, 1).start()
    own_first(1, 0).start()
    own_first(1, 1).start()
    far_copies["up"].start()
    far_copies["down"].start()
    far_copies["own"].start()
    fill(0, 0)
    fill(1, 0)

    def zero(t, carry):
        ob[t] = jnp.zeros((LEAF, 128), F32)
        return carry

    lax.fori_loop(0, 32, zero, 0)

    def own(t, carry):
        g, h = t // 2, t % 2
        add_tile(blk[h, g], g, None, 0)
        rows = pl.ds(pl.multiple_of(g * LEAF, LEAF), LEAF)

        @pl.when(h == 1)
        def _():
            pot[rows, :] = ob[0]
            ob[0] = jnp.zeros((LEAF, 128), F32)

        return carry

    lax.fori_loop(0, 8, own, 0)

    for k in range(2):
        for h in range(2):
            own_first(h, k).wait_recv()
            onward(h, k).start()
            fill(h, 1 if k == 0 else 3)
    for name, more in (("up", ("up2", "side1")), ("down", ("down2", "side3")), ("own", ())):
        far_copies[name].wait_recv()
        for m in more:
            far_copies[m].start()

    def first_tiles(d):
        for h in range(2):
            slot_tiles(h, d, 0, [(j, lambda leaf, b=p1[h][d]: b[leaf]) for j in range(2)])

    def pass_on(d):
        for h in range(2):
            for k in range(2):
                ahead(h, d, k).wait_recv()
                relay(h, d, k).start()

    def second_tiles(d):
        for h in range(2):
            for k in range(2):
                slots(h, d, k).wait_recv()
                slot_tiles(h, d, 1 if k == 0 else 3, [(j, lambda leaf, k=k, j=j: p2[h, d, k, j]) for j in range(2)])

    def relay_tiles(d):
        for h in range(2):
            for k in range(2):
                relay(h, d, k).wait_recv()
            slot_tiles(h, d, 2, [(j, lambda leaf, j=j: p3[h, d, j]) for j in range(2)])

    def far_leaf(g):
        def one(k, q):
            operand = source_operand(fb[far_at[g * 8 + k]], None)
            return q + tile(stgt[g], operand)

        q = lax.fori_loop(0, 8, one, jnp.zeros((HALF, 128), F32))
        rows = pl.ds(g * LEAF, LEAF)
        pot[rows, :] += dot3(interp[rows, :], q)

    pass_on(0)
    for h in range(2):
        onward(h, 0).wait_recv()
        onward(h, 1).wait_recv()
        fill(h, 2)
    far_copies["up2"].wait_recv()
    far_copies["down2"].wait_recv()
    far_copies["side2"].start()
    first_tiles(1)
    first_tiles(3)
    for name in ("side1", "side3", "side2"):
        far_copies[name].wait_recv()
    second_tiles(0)
    pass_on(1)
    far_leaf(0)
    pass_on(3)
    far_leaf(1)
    pass_on(2)
    first_tiles(2)
    far_leaf(2)
    far_leaf(3)
    second_tiles(1)
    second_tiles(3)
    relay_tiles(0)
    second_tiles(2)
    relay_tiles(1)
    relay_tiles(3)
    relay_tiles(2)

    def finish(g, carry):
        rows = pl.ds(pl.multiple_of(g * LEAF, LEAF), LEAF)
        total = pot[rows, :]
        for k in range(7):
            total = total + ob[near_at[g * 7 + k]]
        pot[rows, :] = total
        return carry

    lax.fori_loop(0, 4, finish, 0)

    for h in range(2):
        for k in range(2):
            own_first(h, k).wait_send()
            onward(h, k).wait_send()
            for d in range(4):
                slots(h, d, k).wait_send()
                ahead(h, d, k).wait_send()
                relay(h, d, k).wait_send()
    for one in far_copies.values():
        one.wait_send()


def exchange(code, near_at, far_at, blk, fblk, tgt, stgt, interp):
    dma = pltpu.SemaphoreType.DMA
    return pl.pallas_call(
        exchange_kernel,
        out_shape=jax.ShapeDtypeStruct((ROWS, RHS), F32),
        in_specs=[sspec()] * 3 + [vspec()] * 5,
        out_specs=vspec(),
        scratch_shapes=[pltpu.VMEM((4, BLK, 128), F32)] * 6
        + [
            pltpu.VMEM((2, 4, 2, 3, BLK, 128), F32),
            pltpu.VMEM((2, 4, 2, 3, BLK, 128), F32),
            pltpu.VMEM((2, 4, 2, BLK, 128), F32),
            pltpu.VMEM((28, BLK, 128), F32),
            pltpu.VMEM((32, LEAF, 128), F32),
            dma((2, 4)),
            dma((2, 4)),
        ]
        + [dma((2, 4, 2))] * 6
        + [
            dma((8,)),
            dma((8,)),
        ],
        compiler_params=pltpu.CompilerParams(
            vmem_limit_bytes=VMEM_LIMIT, collective_id=0, has_side_effects=True
        ),
    )(code, near_at, far_at, blk, fblk, tgt, stgt, interp)


def gather_kernel(idx_ref, src_ref, dst_ref):
    def body(b, carry):
        first = pl.multiple_of(b * 16, 16)
        rows = [src_ref[pl.ds(idx_ref[first + u], 1), :] for u in range(16)]
        for u in range(16):
            dst_ref[pl.ds(first + u, 1), :] = rows[u]
        return carry

    lax.fori_loop(0, ROWS // 16, body, 0)


def gather_rows(idx, src):
    return pl.pallas_call(
        gather_kernel,
        out_shape=jax.ShapeDtypeStruct((ROWS, RHS), F32),
        in_specs=[sspec(), vspec()],
        out_specs=vspec(),
        compiler_params=pltpu.CompilerParams(vmem_limit_bytes=VMEM_LIMIT),
    )(idx, src)


def tables(near, far):
    o, i = lax.axis_index("outer"), lax.axis_index("inner")
    y, c, x, z = o // 2, o % 2, i // 4, i % 4
    rows = lax.dynamic_slice_in_dim(near, o * 64, 64, 0)
    entry = rows[:, 1:].reshape(16, 28)
    src, leaf = (entry // 4) % 16, entry % 4
    target = jnp.arange(28, dtype=I32) // 7
    earlier = jnp.arange(28)[:, None] > jnp.arange(28)[None, :]
    nth = jnp.sum(((src[:, :, None] == src[:, None, :]) & earlier[None]).astype(I32), axis=2)
    mark = 16 + 4 * target[None, :] + leaf
    place = src * 2 + nth
    hit = place[:, :, None] == jnp.arange(32, dtype=I32)[None, None, :]
    code = jnp.sum(jnp.where(hit, mark[:, :, None], 0), axis=1).reshape(512)
    mine = lax.dynamic_slice_in_dim(src, i, 1, 0)[0]
    mine_nth = lax.dynamic_slice_in_dim(nth, i, 1, 0)[0]
    near_at = (((x - mine // 4) % 4) * 4 + (z - mine % 4) % 4) * 2 + mine_nth
    f = lax.dynamic_slice_in_dim(far, (o * 16 + i) * 4, 4, 0).reshape(32)
    fo = f // 64
    far_at = (((y - fo // 2) % 4) * 2 + (c + fo) % 2 - 1) * 4 + f % 4
    return code.astype(I32), near_at.astype(I32), far_at.astype(I32)


def shards(points, charges, interp, order, near, far, skel):
    axes = ("outer", "inner")
    code, near_at, far_at = tables(near, far)
    rank, slot = (v.reshape(ROWS) for v in rank_rows(order))
    sent = pack_rows(slot, order, points, charges).reshape(DEVS, 32, 128)
    got = lax.all_to_all(sent, axes, split_axis=0, concat_axis=0, tiled=True)
    pos = got[:, 16:32, DIM].astype(I32).reshape(ROWS)
    blk, fblk, tgt, stgt = place_rows(pos, skel, got, interp)
    pot = exchange(code, near_at, far_at, blk, fblk, tgt, stgt, interp)
    back = gather_rows(pos, pot).reshape(DEVS, 16, RHS)
    back = lax.all_to_all(back, axes, split_axis=0, concat_axis=0, tiled=True)
    return gather_rows(rank, back.reshape(ROWS, RHS))


def solution(mesh):
    rows = P(("outer", "inner"), None)
    return jax.shard_map(
        shards,
        mesh=mesh,
        in_specs=(rows, rows, rows, P(("outer", "inner")), P(), P(), rows),
        out_specs=rows,
        check_vma=False,
    )
```

```python
import functools
import math

import jax
import jax.numpy as jnp
from jax import lax
from jax.experimental import pallas as pl
from jax.experimental.pallas import tpu as pltpu
from jax.sharding import PartitionSpec as P

F32, BF16, I32 = jnp.float32, jnp.bfloat16, jnp.int32
MESH = pl.DeviceIdType.MESH
VMEM_LIMIT = 60 * 1024 * 1024

ROWS = 2048
DEVS = 128
LEAF = 512
HALF = 256
DIM = 64
RHS = 128
BLK = HALF + 128
SCALE = math.log2(math.e) * 4.0 / DIM


def vspec():
    return pl.BlockSpec(memory_space=pltpu.VMEM)


def sspec():
    return pl.BlockSpec(memory_space=pltpu.SMEM)


def dot(a, b, contract=((1,), (0,))):
    return lax.dot_general(a, b, (contract, ((), ())), preferred_element_type=F32)


def hi_lo(v):
    hi = v.astype(BF16)
    return hi, (v - hi.astype(F32)).astype(BF16)


def dot3(a, b, contract=((1,), (0,))):
    ah, al = hi_lo(a)
    bh, bl = hi_lo(b)
    return dot(ah, bh, contract) + dot(ah, bl, contract) + dot(al, bh, contract)


def three(v):
    hi = v.astype(BF16).astype(F32)
    rest = v - hi
    mid = rest.astype(BF16).astype(F32)
    return hi, mid, rest - mid


def plan_kernel(order_ref, near_ref, far_ref, rank_ref, slot_ref, posmat_ref, code_ref, near_at_ref, far_at_ref):
    sub = lax.broadcasted_iota(I32, (128, 128), 0)
    lane = lax.broadcasted_iota(I32, (128, 128), 1)
    before = (sub < lane).astype(F32).astype(BF16)
    ones = jnp.ones((128, 128), BF16)
    base = jnp.zeros((128, 128), F32)
    posmat = jnp.zeros((256, 16), F32)
    for r in range(ROWS // 128):
        order = order_ref[r : r + 1, :]
        owner = order >> 11
        hit = (sub == owner).astype(F32)
        hit16 = hit.astype(BF16)
        seen = dot(hit16, before) + base
        base = base + dot(hit16, ones)
        nth = jnp.sum(hit * seen, axis=0, keepdims=True).astype(I32)
        rank_ref[r : r + 1, :] = owner * 16 + nth
        slot_ref[r : r + 1, :] = owner * 32 + nth
        pos = ((order >> 8) & 1) * 1024 + ((order >> 9) & 3) * HALF + (order & 255)
        slot = (sub[0:16] == nth).astype(F32).astype(BF16)
        high = (hit * (pos >> 4).astype(F32)).astype(BF16)
        low = (hit * (pos & 15).astype(F32)).astype(BF16)
        posmat = posmat + dot(jnp.concatenate([high, low], axis=0), slot, ((1,), (1,)))
    posmat = 16.0 * posmat[0:128] + posmat[128:256]
    posmat_ref[...] = jnp.concatenate([posmat, jnp.zeros((128, 112), F32)], axis=1)

    o, i = lax.axis_index("outer"), lax.axis_index("inner")
    y, c, x, z = o >> 1, o & 1, i >> 2, i & 3
    entry = near_ref[...]
    row = lax.broadcasted_iota(I32, entry.shape, 0)
    g = lax.broadcasted_iota(I32, entry.shape, 1) & 3
    src = jnp.where(row == 0, -1, (entry >> 2) & 15)
    nth = jnp.zeros(entry.shape, I32)
    for back in range(4):
        other = src if back == 0 else pltpu.roll(src, back, axis=1)
        for k in range(1, 8):
            earlier = (row > k) if back == 0 else (g >= back)
            nth = nth + jnp.where((other[k : k + 1, :] == src) & earlier, 1, 0)
    place = src * 2 + nth
    mark = 16 + 4 * g + (entry & 3)
    want = lax.broadcasted_iota(I32, (32, entry.shape[1]), 0)
    code = jnp.zeros(want.shape, I32)
    for k in range(1, 8):
        code = code + jnp.where(want == place[k : k + 1, :], mark[k : k + 1, :], 0)
    n = code.shape[1]
    code = code + pltpu.roll(code, n - 1, axis=1)
    code_ref[...] = code + pltpu.roll(code, n - 2, axis=1)
    near_at_ref[...] = ((((x - (src >> 2)) & 3) * 4 + ((z - src) & 3)) * 2 + nth) & 31
    f = far_ref[...]
    fo = f >> 6
    far_at_ref[...] = ((((y - (fo >> 1)) & 3) * 2 + ((c + fo) & 1)) - 1) * 4 + (f & 3)


def make_plan(order, near, far):
    leaves = near.shape[0]
    sd = jax.ShapeDtypeStruct
    return pl.pallas_call(
        plan_kernel,
        out_shape=[sd((ROWS // 128, 128), I32)] * 2
        + [sd((DEVS, 128), F32), sd((32, leaves), I32), sd((8, leaves), I32), sd((8, leaves), I32)],
        in_specs=[vspec()] * 3,
        out_specs=[vspec()] * 6,
    )(order.reshape(ROWS // 128, 128), near.T, far.T)


SENT = 25


def send_kernel(rank_ref, slot_ref, pts_ref, chg_ref, posmat_ref, sent_ref, wide, ranked):
    for r in range(ROWS // 128):
        x = pts_ref[:, r * 128 : (r + 1) * 128]
        wide[r * 128 : (r + 1) * 128, :] = jnp.transpose(jnp.concatenate([x, x], axis=0))

    def body(b, carry):
        first = pl.multiple_of(b * 16, 16)
        to = [slot_ref[first + u] for u in range(16)]
        at = [rank_ref[first + u] for u in range(16)]
        chg = [chg_ref[pl.ds(first + u, 1), :] for u in range(16)]
        pts = [wide[pl.ds(first + u, 1), :] for u in range(16)]
        for u in range(16):
            sent_ref[pl.ds(to[u], 1), :] = chg[u]
            ranked[pl.ds(at[u], 1), :] = pts[u]
        return carry

    lax.fori_loop(0, ROWS // 16, body, 0)
    left = lax.broadcasted_iota(I32, (8, 128), 1) < DIM

    def pack(b, carry):
        for u in range(8):
            d = b * 8 + u
            low = ranked[pl.ds(pl.multiple_of(d * 16, 8), 8), :]
            high = ranked[pl.ds(pl.multiple_of(d * 16 + 8, 8), 8), :]
            sent_ref[pl.ds(pl.multiple_of(d * 32 + 16, 8), 8), :] = jnp.where(left, low, high)
            sent_ref[pl.ds(d * 32 + 24, 1), :] = posmat_ref[pl.ds(d, 1), :]
        return carry

    lax.fori_loop(0, DEVS // 8, pack, 0)


def pack_rows(rank, slot, points, charges, posmat):
    return pl.pallas_call(
        send_kernel,
        out_shape=jax.ShapeDtypeStruct((DEVS * 32, 128), F32),
        in_specs=[sspec(), sspec(), vspec(), vspec(), vspec()],
        out_specs=vspec(),
        scratch_shapes=[pltpu.VMEM((ROWS, 128), F32)] * 2,
        compiler_params=pltpu.CompilerParams(vmem_limit_bytes=VMEM_LIMIT),
    )(rank, slot, points.T, charges, posmat)


def peer(t):
    o, i = lax.axis_index("outer"), lax.axis_index("inner")
    y, c, x, z = o >> 1, o & 1, i >> 2, i & 3
    a, b, e, other = t & 3, (t >> 2) & 3, (t >> 4) & 3, t >> 6
    return ((((y + a) & 3) << 1) | (c ^ other), (((x + a + b) & 3) << 2) | ((z + e + 3 * a) & 3))


def greet_all():
    barrier = pltpu.get_barrier_semaphore()

    def greet(t, carry):
        pl.semaphore_signal(barrier, inc=1, device_id=peer(t), device_id_type=MESH)
        return carry

    lax.fori_loop(1, DEVS, greet, 0)
    pl.semaphore_wait(barrier, DEVS - 1)


def out_kernel(src, dst, pos, send, recv, own):
    me = lax.axis_index("outer") * 16 + lax.axis_index("inner")
    rows = pl.ds(0, SENT)
    keep = pltpu.make_async_copy(src.at[me, rows], dst.at[me, rows], own)
    keep.start()
    greet_all()

    def go(t, carry):
        to = peer(t)
        pltpu.make_async_remote_copy(
            src_ref=src.at[to[0] * 16 + to[1], rows], dst_ref=dst.at[me, rows], send_sem=send, recv_sem=recv,
            device_id=to, device_id_type=MESH,
        ).start()
        return carry

    lax.fori_loop(1, DEVS, go, 0)
    most = pl.ds(0, DEVS - 1)
    whole = pltpu.make_async_remote_copy(
        src_ref=src.at[most, rows], dst_ref=dst.at[most, rows], send_sem=send, recv_sem=recv,
        device_id=peer(1), device_id_type=MESH,
    )
    keep.wait()
    whole.wait_recv()
    pos[...] = dst[:, 24, :].astype(I32)
    whole.wait_send()


def rows_out(sent):
    dma = pltpu.SemaphoreType.DMA
    return pl.pallas_call(
        out_kernel,
        out_shape=[jax.ShapeDtypeStruct((DEVS, 32, 128), F32), jax.ShapeDtypeStruct((DEVS, 128), I32)],
        in_specs=[vspec()],
        out_specs=[vspec()] * 2,
        scratch_shapes=[dma, dma, dma],
        compiler_params=pltpu.CompilerParams(vmem_limit_bytes=VMEM_LIMIT, collective_id=1, has_side_effects=True),
    )(sent.reshape(DEVS, 32, 128))


def place_kernel(pos_ref, got_ref, blk_ref, pts_ref, turned):
    def turn(b, carry):
        for u in range(8):
            d = b * 8 + u
            rows = got_ref[pl.ds(pl.multiple_of(d * 32 + 16, 8), 8), :]
            turned[pl.ds(pl.multiple_of(d * 8, 8), 8), :] = pltpu.roll(rows, DIM, axis=1)
        return carry

    lax.fori_loop(0, DEVS // 8, turn, 0)

    def place(b, carry):
        at = [pos_ref[b, u] for u in range(16)]
        row = [a + ((a >> 8) << 7) for a in at]
        base = pl.multiple_of(b * 32, 32)
        half = pl.multiple_of(b * 8, 8)
        c = [got_ref[pl.ds(base + u, 1), :] for u in range(16)]
        p = [got_ref[pl.ds(base + 16 + u, 1), :] for u in range(8)] + [turned[pl.ds(half + u, 1), :] for u in range(8)]
        for u in range(16):
            blk_ref[pl.ds(row[u], 1), :] = c[u]
            pts_ref[pl.ds(at[u], 1), :] = p[u]
        return carry

    lax.fori_loop(0, DEVS, place, 0)
    for k in range(8):
        xt = jnp.transpose(pts_ref[k * HALF : (k + 1) * HALF, :])
        blk_ref[k * BLK + HALF : k * BLK + HALF + 64, :] = xt[0:64, 0:128]
        blk_ref[k * BLK + HALF + 64 : (k + 1) * BLK, :] = xt[0:64, 128:256]


def place_rows(pos, got):
    blk, pts = pl.pallas_call(
        place_kernel,
        out_shape=[jax.ShapeDtypeStruct((8 * BLK, 128), F32), jax.ShapeDtypeStruct((ROWS, 128), F32)],
        in_specs=[sspec(), vspec()],
        out_specs=[vspec()] * 2,
        scratch_shapes=[pltpu.VMEM((DEVS * 8, 128), F32)],
        compiler_params=pltpu.CompilerParams(vmem_limit_bytes=VMEM_LIMIT),
    )(pos, got.reshape(DEVS * 32, 128))
    return blk.reshape(2, 4, BLK, 128), pts


def target_operand(x):
    n = x.shape[0]
    hi, lo = hi_lo(x * (2.0 * SCALE))
    norm = jnp.sum(x * x, axis=1, keepdims=True) * (-SCALE)
    n0, n1, n2 = three(norm)
    lane = lax.broadcasted_iota(I32, (n, DIM), 1)
    tail = jnp.where(
        lane == 0, n0, jnp.where(lane == 1, n1, jnp.where(lane == 2, n2, jnp.where(lane < 6, 1.0, 0.0)))
    )
    return jnp.concatenate([hi, hi, lo, tail.astype(BF16)], axis=1)


def source_operand(block, scale):
    xt = jnp.concatenate([block[HALF : HALF + 64, :], block[HALF + 64 : BLK, :]], axis=1)
    hi, lo = hi_lo(xt)
    norm = jnp.sum(xt * xt, axis=0, keepdims=True) * (-SCALE)
    n0, n1, n2 = three(norm)
    row = lax.broadcasted_iota(I32, (16, HALF), 0)
    tail = jnp.where(
        row < 3, 1.0, jnp.where(row == 3, n0, jnp.where(row == 4, n1, jnp.where(row == 5, n2, 0.0)))
    )
    right = jnp.concatenate([hi, lo, hi, tail.astype(BF16), jnp.zeros((48, HALF), BF16)], axis=0)
    chg = block[0:HALF, :]
    if scale is not None:
        chg = chg * scale
    ch, cl = hi_lo(chg)
    return right, jnp.concatenate([ch, cl], axis=1)


def tile(target, operand):
    right, both = operand
    n = target.shape[0]
    g = jnp.exp2(dot(target, right))
    gh, gl = hi_lo(g)
    wide = dot(jnp.concatenate([gh, gl], axis=0), both)
    return wide[:n, 0:128] + (wide[:n, 128:256] + wide[n:, 0:128])


def exchange_kernel(
    code, near_at, far_at, skel, blk, pts, interp, pot,
    fblk, tgt, stgt, sk, p1a1, p1a2, p1a3, p1b1, p1b2, p1b3, sb, p2, p3, fb, ob,
    s1, r1, s2, r2, s3, r3, s4, r4, sf, rf,
):
    o, i = lax.axis_index("outer"), lax.axis_index("inner")
    y, c, x, z = o // 2, o % 2, i // 4, i % 4
    p1 = ((None, p1a1, p1a2, p1a3), (None, p1b1, p1b2, p1b3))

    def at_inner(dx, dz):
        return ((x + dx + 4) % 4) * 4 + (z + dz + 4) % 4

    def off(h, d1, d2):
        return at_inner(d1, d2) if h == 0 else at_inner(d2, d1)

    def first(h, d):
        return (o, off(h, d, 0))

    def second(h, d):
        return (o, off(h, 0, d))

    def along_y(d):
        return (((y + d + 4) % 4) * 2 + c, i)

    sibling = (y * 2 + 1 - c, i)
    mine = (o * 16 + i) * 4

    barrier = pltpu.get_barrier_semaphore()
    peers = [first(0, 1), first(0, -1), second(0, 1), second(0, -1), along_y(1), along_y(-1), sibling]
    for peer in peers:
        pl.semaphore_signal(barrier, inc=1, device_id=peer, device_id_type=MESH)
    pl.semaphore_wait(barrier, len(peers))

    def copy(src, dst, send, recv, to):
        return pltpu.make_async_remote_copy(
            src_ref=src, dst_ref=dst, send_sem=send, recv_sem=recv, device_id=to, device_id_type=MESH
        )

    def own_first(h, k):
        return copy(blk.at[h], p1[h][1 if k == 0 else 3], s1.at[h, k], r1.at[h, k], first(h, 1 if k == 0 else -1))

    def onward(h, k):
        part = pl.ds(2 * k, 2)
        src = p1[h][1 if k == 0 else 3].at[part]
        return copy(src, p1[h][2].at[part], s1.at[h, 2 + k], r1.at[h, 2 + k], first(h, 1 if k == 0 else -1))

    def slots(h, d, k):
        two = pl.ds(0, 2)
        to = second(h, 1 if k == 0 else -1)
        return copy(sb.at[h, d, k, two], p2.at[h, d, k, two], s2.at[h, d, k], r2.at[h, d, k], to)

    def ahead(h, d, k):
        to = second(h, 1 if k == 0 else -1)
        return copy(sb.at[h, d, k, 2], p2.at[h, d, k, 2], s4.at[h, d, k], r4.at[h, d, k], to)

    def relay(h, d, k):
        return copy(p2.at[h, d, k, 2], p3.at[h, d, k], s3.at[h, d, k], r3.at[h, d, k], second(h, 1 if k == 0 else -1))

    def fbuf(dy, dc, lo=0, n=4):
        return fb.at[pl.ds((dy * 2 + dc - 1) * 4 + lo, n)]

    far_copies = {
        "up": copy(fblk, fbuf(1, 0), sf.at[0], rf.at[0], along_y(1)),
        "down": copy(fblk, fbuf(3, 0), sf.at[1], rf.at[1], along_y(-1)),
        "own": copy(fblk, fbuf(0, 1), sf.at[2], rf.at[2], sibling),
        "up2": copy(fbuf(1, 0, 0, 2), fbuf(2, 0, 0, 2), sf.at[3], rf.at[3], along_y(1)),
        "down2": copy(fbuf(3, 0, 2, 2), fbuf(2, 0, 2, 2), sf.at[4], rf.at[4], along_y(-1)),
        "side1": copy(fbuf(1, 0), fbuf(1, 1), sf.at[5], rf.at[5], sibling),
        "side3": copy(fbuf(3, 0), fbuf(3, 1), sf.at[6], rf.at[6], sibling),
        "side2": copy(fbuf(2, 0), fbuf(2, 1), sf.at[7], rf.at[7], sibling),
    }

    def leaf_code(dest, src, j):
        return code[src * 2 + j, (o * 16 + dest) * 4]

    def fill(h, d):
        src = off(h, -d, 0)
        for k in range(2):
            for slot in (2, 0, 1):
                dest = off(h, 0, (1 if k == 0 else -1) if slot < 2 else 2)
                leaf = leaf_code(dest, src, slot if slot < 2 else k) % 4
                if d == 0:
                    sb[h, d, k, slot] = blk[h, leaf]
                else:
                    sb[h, d, k, slot] = p1[h][d][leaf]
                if slot == 2:
                    ahead(h, d, k).start()
            slots(h, d, k).start()

    def add_tile(block, g, scale, at):
        ob[at] += tile(tgt[g], source_operand(block, scale))

    def slot_tiles(h, d, e, which):
        dx, dz = (d, e) if h == 0 else (e, d)
        src = at_inner(-dx, -dz)
        for j, load in which:
            v = leaf_code(i, src, j)
            add_tile(load(v % 4), (v // 4) % 4, (v // 16).astype(F32), (dx * 4 + dz) * 2 + j)

    own_first(0, 0).start()
    own_first(0, 1).start()
    own_first(1, 0).start()
    own_first(1, 1).start()
    fill(0, 0)
    fill(1, 0)

    for g in range(4):
        def pick(b, carry, g=g):
            rows = []
            for u in range(16):
                q = skel[g, b * 16 + u]
                rows.append(pts[pl.ds((q >> 8) * 1024 + g * HALF + (q & 255), 1), :])
            for u in range(16):
                sk[pl.ds(b * 16 + u, 1), :] = rows[u]
            return carry

        lax.fori_loop(0, 16, pick, 0)
        skt = jnp.transpose(sk[...])
        fblk[g, HALF : HALF + 64, :] = skt[0:64, 0:128]
        fblk[g, HALF + 64 : BLK, :] = skt[0:64, 128:256]
        stgt[g] = target_operand(sk[:, 0:DIM])
        charges = jnp.zeros((HALF, RHS), F32)
        for h in range(2):
            tgt[g, h * HALF : (h + 1) * HALF, :] = target_operand(pts[h * 1024 + g * HALF : h * 1024 + (g + 1) * HALF, 0:DIM])
            weights = interp[g * LEAF + h * HALF : g * LEAF + (h + 1) * HALF, :]
            charges = charges + dot3(weights, blk[h, g, 0:HALF, :], ((0,), (0,)))
        fblk[g, 0:HALF, :] = charges
    far_copies["up"].start()
    far_copies["down"].start()
    far_copies["own"].start()

    def halves(g):
        return [pl.ds(pl.multiple_of(h * 1024 + g * HALF, HALF), HALF) for h in range(2)]

    def put(g, values):
        for h, rows in enumerate(halves(g)):
            pot[rows, :] = values[h * HALF : (h + 1) * HALF, :]

    def zero(t, carry):
        ob[t] = jnp.zeros((LEAF, 128), F32)
        return carry

    lax.fori_loop(0, 32, zero, 0)

    def own(t, carry):
        g, h = t // 2, t % 2
        add_tile(blk[h, g], g, None, 0)

        @pl.when(h == 1)
        def _():
            put(g, ob[0])
            ob[0] = jnp.zeros((LEAF, 128), F32)

        return carry

    lax.fori_loop(0, 8, own, 0)

    for k in range(2):
        for h in range(2):
            own_first(h, k).wait_recv()
            onward(h, k).start()
            fill(h, 1 if k == 0 else 3)
    for name, more in (("up", ("up2", "side1")), ("down", ("down2", "side3")), ("own", ())):
        far_copies[name].wait_recv()
        for m in more:
            far_copies[m].start()

    def first_tiles(d):
        for h in range(2):
            slot_tiles(h, d, 0, [(j, lambda leaf, b=p1[h][d]: b[leaf]) for j in range(2)])

    def pass_on(d):
        for h in range(2):
            for k in range(2):
                ahead(h, d, k).wait_recv()
                relay(h, d, k).start()

    def second_tiles(d):
        for h in range(2):
            for k in range(2):
                slots(h, d, k).wait_recv()
                slot_tiles(h, d, 1 if k == 0 else 3, [(j, lambda leaf, k=k, j=j: p2[h, d, k, j]) for j in range(2)])

    def relay_tiles(d):
        for h in range(2):
            for k in range(2):
                relay(h, d, k).wait_recv()
            slot_tiles(h, d, 2, [(j, lambda leaf, j=j: p3[h, d, j]) for j in range(2)])

    def far_leaf(g):
        def one(k, q):
            operand = source_operand(fb[far_at[k, mine + g]], None)
            return q + tile(stgt[g], operand)

        q = lax.fori_loop(0, 8, one, jnp.zeros((HALF, 128), F32))
        more = dot3(interp[g * LEAF : (g + 1) * LEAF, :], q)
        for h, rows in enumerate(halves(g)):
            pot[rows, :] += more[h * HALF : (h + 1) * HALF, :]

    pass_on(0)
    for h in range(2):
        onward(h, 0).wait_recv()
        onward(h, 1).wait_recv()
        fill(h, 2)
    far_copies["up2"].wait_recv()
    far_copies["down2"].wait_recv()
    far_copies["side2"].start()
    first_tiles(1)
    first_tiles(3)
    for name in ("side1", "side3", "side2"):
        far_copies[name].wait_recv()
    second_tiles(0)
    pass_on(1)
    far_leaf(0)
    pass_on(3)
    far_leaf(1)
    pass_on(2)
    first_tiles(2)
    far_leaf(2)
    far_leaf(3)
    second_tiles(1)
    second_tiles(3)
    relay_tiles(0)
    second_tiles(2)
    relay_tiles(1)
    relay_tiles(3)
    relay_tiles(2)

    def finish(g, carry):
        at = [near_at[k + 1, mine + g] for k in range(7)]
        for h, rows in enumerate(halves(g)):
            total = pot[rows, :]
            for k in range(7):
                total = total + ob[at[k], h * HALF : (h + 1) * HALF, :]
            pot[rows, :] = total
        return carry

    lax.fori_loop(0, 4, finish, 0)

    for h in range(2):
        for k in range(2):
            own_first(h, k).wait_send()
            onward(h, k).wait_send()
            for d in range(4):
                slots(h, d, k).wait_send()
                ahead(h, d, k).wait_send()
                relay(h, d, k).wait_send()
    for one in far_copies.values():
        one.wait_send()


def exchange(code, near_at, far_at, skel, blk, pts, interp):
    dma = pltpu.SemaphoreType.DMA
    return pl.pallas_call(
        exchange_kernel,
        out_shape=jax.ShapeDtypeStruct((ROWS, RHS), F32),
        in_specs=[sspec()] * 4 + [vspec()] * 3,
        out_specs=vspec(),
        scratch_shapes=[
            pltpu.VMEM((4, BLK, 128), F32),
            pltpu.VMEM((4, LEAF, 256), BF16),
            pltpu.VMEM((4, HALF, 256), BF16),
            pltpu.VMEM((HALF, 128), F32),
        ]
        + [pltpu.VMEM((4, BLK, 128), F32)] * 6
        + [
            pltpu.VMEM((2, 4, 2, 3, BLK, 128), F32),
            pltpu.VMEM((2, 4, 2, 3, BLK, 128), F32),
            pltpu.VMEM((2, 4, 2, BLK, 128), F32),
            pltpu.VMEM((28, BLK, 128), F32),
            pltpu.VMEM((32, LEAF, 128), F32),
            dma((2, 4)),
            dma((2, 4)),
        ]
        + [dma((2, 4, 2))] * 6
        + [
            dma((8,)),
            dma((8,)),
        ],
        compiler_params=pltpu.CompilerParams(
            vmem_limit_bytes=VMEM_LIMIT, collective_id=0, has_side_effects=True
        ),
    )(code, near_at, far_at, skel, blk, pts, interp)


def back_kernel(pos, pot, dst, buf, send, recv):
    me = lax.axis_index("outer") * 16 + lax.axis_index("inner")
    greet_all()

    def choose(d):
        return [pot[pl.ds(pos[d, u], 1), :] for u in range(16)]

    def go(t, carry):
        to = peer(t)
        d = to[0] * 16 + to[1]
        for u, row in enumerate(choose(d)):
            buf[d, u : u + 1, :] = row
        pltpu.make_async_remote_copy(
            src_ref=buf.at[d], dst_ref=dst.at[me], send_sem=send, recv_sem=recv, device_id=to, device_id_type=MESH
        ).start()
        return carry

    lax.fori_loop(1, DEVS, go, 0)
    for u, row in enumerate(choose(me)):
        dst[me, u : u + 1, :] = row
    most = pl.ds(0, DEVS - 1)
    whole = pltpu.make_async_remote_copy(
        src_ref=buf.at[most], dst_ref=dst.at[most], send_sem=send, recv_sem=recv,
        device_id=peer(1), device_id_type=MESH,
    )
    whole.wait_recv()
    whole.wait_send()


def rows_back(pos, pot):
    dma = pltpu.SemaphoreType.DMA
    shape = (DEVS, 16, RHS)
    return pl.pallas_call(
        back_kernel,
        out_shape=jax.ShapeDtypeStruct(shape, F32),
        in_specs=[sspec(), vspec()],
        out_specs=vspec(),
        scratch_shapes=[pltpu.VMEM(shape, F32), dma, dma],
        compiler_params=pltpu.CompilerParams(vmem_limit_bytes=VMEM_LIMIT, collective_id=2, has_side_effects=True),
    )(pos, pot).reshape(ROWS, RHS)


def gather_kernel(idx_ref, src_ref, dst_ref):
    def body(b, carry):
        first = pl.multiple_of(b * 16, 16)
        rows = [src_ref[pl.ds(idx_ref[first + u], 1), :] for u in range(16)]
        for u in range(16):
            dst_ref[pl.ds(first + u, 1), :] = rows[u]
        return carry

    lax.fori_loop(0, ROWS // 16, body, 0)


def gather_rows(idx, src):
    return pl.pallas_call(
        gather_kernel,
        out_shape=jax.ShapeDtypeStruct((ROWS, RHS), F32),
        in_specs=[sspec(), vspec()],
        out_specs=vspec(),
        compiler_params=pltpu.CompilerParams(vmem_limit_bytes=VMEM_LIMIT),
    )(idx, src)


def shards(points, charges, interp, order, near, far, skel):
    rank, slot, posmat, code, near_at, far_at = make_plan(order, near, far)
    rank, slot = rank.reshape(ROWS), slot.reshape(ROWS)
    got, pos = rows_out(pack_rows(rank, slot, points, charges, posmat))
    blk, pts = place_rows(pos, got)
    pot = exchange(code, near_at, far_at, skel, blk, pts, interp)
    return gather_rows(rank, rows_back(pos, pot))


def solution(mesh):
    rows = P(("outer", "inner"), None)
    return jax.shard_map(
        shards,
        mesh=mesh,
        in_specs=(rows, rows, rows, P(("outer", "inner")), P(), P(), rows),
        out_specs=rows,
        check_vma=False,
    )
```

```python
import functools
import math

import jax
import jax.numpy as jnp
from jax import lax
from jax.experimental import pallas as pl
from jax.experimental.pallas import tpu as pltpu
from jax.sharding import PartitionSpec as P

F32, BF16, I32 = jnp.float32, jnp.bfloat16, jnp.int32
MESH = pl.DeviceIdType.MESH
VMEM_LIMIT = 60 * 1024 * 1024

ROWS = 2048
DEVS = 128
LEAF = 512
HALF = 256
DIM = 64
RHS = 128
BLK = HALF + 128
SCALE = math.log2(math.e) * 4.0 / DIM


def vspec():
    return pl.BlockSpec(memory_space=pltpu.VMEM)


def sspec():
    return pl.BlockSpec(memory_space=pltpu.SMEM)


def dot(a, b, contract=((1,), (0,))):
    return lax.dot_general(a, b, (contract, ((), ())), preferred_element_type=F32)


def hi_lo(v):
    hi = v.astype(BF16)
    return hi, (v - hi.astype(F32)).astype(BF16)


def dot3(a, b, contract=((1,), (0,))):
    ah, al = hi_lo(a)
    bh, bl = hi_lo(b)
    return dot(ah, bh, contract) + dot(ah, bl, contract) + dot(al, bh, contract)


def three(v):
    hi = v.astype(BF16).astype(F32)
    rest = v - hi
    mid = rest.astype(BF16).astype(F32)
    return hi, mid, rest - mid


def plan_kernel(order_ref, near_ref, far_ref, sort_ref, posmat_ref, code_ref, near_at_ref, far_at_ref):
    sub = lax.broadcasted_iota(I32, (128, 128), 0)
    lane = lax.broadcasted_iota(I32, (128, 128), 1)
    before = (sub < lane).astype(F32).astype(BF16)
    ones = jnp.ones((128, 128), BF16)
    base = jnp.zeros((128, 128), F32)
    both = jnp.zeros((512, 16), F32)
    for r in range(ROWS // 128):
        order = order_ref[r : r + 1, :]
        owner = order >> 11
        hit = (sub == owner).astype(F32)
        hit16 = hit.astype(BF16)
        seen = dot(hit16, before) + base
        base = base + dot(hit16, ones)
        nth = jnp.sum(hit * seen, axis=0, keepdims=True).astype(I32)
        pos = ((order >> 8) & 1) * 1024 + ((order >> 9) & 3) * HALF + (order & 255)
        slot = (sub[0:16] == nth).astype(F32).astype(BF16)
        row = lane[0:1] + r * 128
        pieces = [(hit * v.astype(F32)).astype(BF16) for v in (pos >> 4, pos & 15, row >> 4, row & 15)]
        both = both + dot(jnp.concatenate(pieces, axis=0), slot, ((1,), (1,)))
    rest = jnp.zeros((128, 112), F32)
    posmat_ref[...] = jnp.concatenate([16.0 * both[0:128] + both[128:256], rest], axis=1)
    sort_ref[...] = jnp.concatenate([16.0 * both[256:384] + both[384:512], rest], axis=1).astype(I32)

    o, i = lax.axis_index("outer"), lax.axis_index("inner")
    y, c, x, z = o >> 1, o & 1, i >> 2, i & 3
    entry = near_ref[...]
    row = lax.broadcasted_iota(I32, entry.shape, 0)
    g = lax.broadcasted_iota(I32, entry.shape, 1) & 3
    src = jnp.where(row == 0, -1, (entry >> 2) & 15)
    nth = jnp.zeros(entry.shape, I32)
    for back in range(4):
        other = src if back == 0 else pltpu.roll(src, back, axis=1)
        for k in range(1, 8):
            earlier = (row > k) if back == 0 else (g >= back)
            nth = nth + jnp.where((other[k : k + 1, :] == src) & earlier, 1, 0)
    place = src * 2 + nth
    mark = 16 + 4 * g + (entry & 3)
    want = lax.broadcasted_iota(I32, (32, entry.shape[1]), 0)
    code = jnp.zeros(want.shape, I32)
    for k in range(1, 8):
        code = code + jnp.where(want == place[k : k + 1, :], mark[k : k + 1, :], 0)
    n = code.shape[1]
    code = code + pltpu.roll(code, n - 1, axis=1)
    code_ref[...] = code + pltpu.roll(code, n - 2, axis=1)
    near_at_ref[...] = ((((x - (src >> 2)) & 3) * 4 + ((z - src) & 3)) * 2 + nth) & 31
    f = far_ref[...]
    fo = f >> 6
    far_at_ref[...] = ((((y - (fo >> 1)) & 3) * 2 + ((c + fo) & 1)) - 1) * 4 + (f & 3)


def make_plan(order, near, far):
    leaves = near.shape[0]
    sd = jax.ShapeDtypeStruct
    return pl.pallas_call(
        plan_kernel,
        out_shape=[
            sd((DEVS, 128), I32),
            sd((DEVS, 128), F32),
            sd((32, leaves), I32),
            sd((8, leaves), I32),
            sd((8, leaves), I32),
        ],
        in_specs=[vspec()] * 3,
        out_specs=[vspec()] * 5,
    )(order.reshape(ROWS // 128, 128), near.T, far.T)


SENT = 25


def peer(t):
    o, i = lax.axis_index("outer"), lax.axis_index("inner")
    y, c, x, z = o >> 1, o & 1, i >> 2, i & 3
    a, b, e, other = t & 3, (t >> 2) & 3, (t >> 4) & 3, t >> 6
    return ((((y + a) & 3) << 1) | (c ^ other), (((x + a + b) & 3) << 2) | ((z + e + 3 * a) & 3))


def greet_all():
    def greet(t, carry):
        pl.semaphore_signal(pltpu.get_barrier_semaphore(), inc=1, device_id=peer(t), device_id_type=MESH)
        return carry

    lax.fori_loop(1, DEVS, greet, 0)


def out_kernel(sort, posmat, pts, chg, dst, pos, wide, buf, send, recv):
    me = lax.axis_index("outer") * 16 + lax.axis_index("inner")
    rows = pl.ds(0, SENT)
    greet_all()
    for r in range(ROWS // 128):
        x = pts[:, r * 128 : (r + 1) * 128]
        wide[r * 128 : (r + 1) * 128, :] = jnp.transpose(jnp.concatenate([x, x], axis=0))
    left = lax.broadcasted_iota(I32, (1, 128), 1) < DIM

    def fill(ref, d):
        at = [sort[d, u] for u in range(16)]
        c = [chg[pl.ds(n, 1), :] for n in at]
        p = [wide[pl.ds(n, 1), :] for n in at]
        for u in range(16):
            ref[d, u : u + 1, :] = c[u]
        for u in range(8):
            ref[d, 16 + u : 17 + u, :] = jnp.where(left, p[u], p[u + 8])
        ref[d, 24:25, :] = posmat[pl.ds(d, 1), :]

    fill(dst, me)
    pl.semaphore_wait(pltpu.get_barrier_semaphore(), DEVS - 1)

    def go(t, carry):
        to = peer(t)
        d = to[0] * 16 + to[1]
        fill(buf, d)
        pltpu.make_async_remote_copy(
            src_ref=buf.at[d, rows], dst_ref=dst.at[me, rows], send_sem=send, recv_sem=recv,
            device_id=to, device_id_type=MESH,
        ).start()
        return carry

    lax.fori_loop(1, DEVS, go, 0)
    most = pl.ds(0, DEVS - 1)
    whole = pltpu.make_async_remote_copy(
        src_ref=buf.at[most, rows], dst_ref=dst.at[most, rows], send_sem=send, recv_sem=recv,
        device_id=peer(1), device_id_type=MESH,
    )
    whole.wait_recv()
    pos[...] = dst[:, 24, :].astype(I32)
    whole.wait_send()


def rows_out(sort, posmat, points, charges):
    dma = pltpu.SemaphoreType.DMA
    return pl.pallas_call(
        out_kernel,
        out_shape=[jax.ShapeDtypeStruct((DEVS, 32, 128), F32), jax.ShapeDtypeStruct((DEVS, 128), I32)],
        in_specs=[sspec(), vspec(), vspec(), vspec()],
        out_specs=[vspec()] * 2,
        scratch_shapes=[pltpu.VMEM((ROWS, 128), F32), pltpu.VMEM((DEVS, 32, 128), F32), dma, dma],
        compiler_params=pltpu.CompilerParams(vmem_limit_bytes=VMEM_LIMIT, collective_id=1, has_side_effects=True),
    )(sort, posmat, points.T, charges)


def place_kernel(pos_ref, got_ref, blk_ref, pts_ref, turned):
    def turn(b, carry):
        for u in range(8):
            d = b * 8 + u
            rows = got_ref[pl.ds(pl.multiple_of(d * 32 + 16, 8), 8), :]
            turned[pl.ds(pl.multiple_of(d * 8, 8), 8), :] = pltpu.roll(rows, DIM, axis=1)
        return carry

    lax.fori_loop(0, DEVS // 8, turn, 0)

    def place(b, carry):
        at = [pos_ref[b, u] for u in range(16)]
        row = [a + ((a >> 8) << 7) for a in at]
        base = pl.multiple_of(b * 32, 32)
        half = pl.multiple_of(b * 8, 8)
        c = [got_ref[pl.ds(base + u, 1), :] for u in range(16)]
        p = [got_ref[pl.ds(base + 16 + u, 1), :] for u in range(8)] + [turned[pl.ds(half + u, 1), :] for u in range(8)]
        for u in range(16):
            blk_ref[pl.ds(row[u], 1), :] = c[u]
            pts_ref[pl.ds(at[u], 1), :] = p[u]
        return carry

    lax.fori_loop(0, DEVS, place, 0)
    for k in range(8):
        xt = jnp.transpose(pts_ref[k * HALF : (k + 1) * HALF, :])
        blk_ref[k * BLK + HALF : k * BLK + HALF + 64, :] = xt[0:64, 0:128]
        blk_ref[k * BLK + HALF + 64 : (k + 1) * BLK, :] = xt[0:64, 128:256]


def place_rows(pos, got):
    blk, pts = pl.pallas_call(
        place_kernel,
        out_shape=[jax.ShapeDtypeStruct((8 * BLK, 128), F32), jax.ShapeDtypeStruct((ROWS, 128), F32)],
        in_specs=[sspec(), vspec()],
        out_specs=[vspec()] * 2,
        scratch_shapes=[pltpu.VMEM((DEVS * 8, 128), F32)],
        compiler_params=pltpu.CompilerParams(vmem_limit_bytes=VMEM_LIMIT),
    )(pos, got.reshape(DEVS * 32, 128))
    return blk.reshape(2, 4, BLK, 128), pts


def target_operand(x):
    n = x.shape[0]
    hi, lo = hi_lo(x * (2.0 * SCALE))
    norm = jnp.sum(x * x, axis=1, keepdims=True) * (-SCALE)
    n0, n1, n2 = three(norm)
    lane = lax.broadcasted_iota(I32, (n, DIM), 1)
    tail = jnp.where(
        lane == 0, n0, jnp.where(lane == 1, n1, jnp.where(lane == 2, n2, jnp.where(lane < 6, 1.0, 0.0)))
    )
    return jnp.concatenate([hi, hi, lo, tail.astype(BF16)], axis=1)


def source_operand(block, scale):
    xt = jnp.concatenate([block[HALF : HALF + 64, :], block[HALF + 64 : BLK, :]], axis=1)
    hi, lo = hi_lo(xt)
    norm = jnp.sum(xt * xt, axis=0, keepdims=True) * (-SCALE)
    n0, n1, n2 = three(norm)
    row = lax.broadcasted_iota(I32, (16, HALF), 0)
    tail = jnp.where(
        row < 3, 1.0, jnp.where(row == 3, n0, jnp.where(row == 4, n1, jnp.where(row == 5, n2, 0.0)))
    )
    right = jnp.concatenate([hi, lo, hi, tail.astype(BF16), jnp.zeros((48, HALF), BF16)], axis=0)
    chg = block[0:HALF, :]
    if scale is not None:
        chg = chg * scale
    ch, cl = hi_lo(chg)
    return right, jnp.concatenate([ch, cl], axis=1)


def tile(target, operand):
    right, both = operand
    n = target.shape[0]
    g = jnp.exp2(dot(target, right))
    gh, gl = hi_lo(g)
    wide = dot(jnp.concatenate([gh, gl], axis=0), both)
    return wide[:n, 0:128] + (wide[:n, 128:256] + wide[n:, 0:128])


CHAIN = ((0, 0), (1, 0), (1, 1), (2, 1), (2, 2), (3, 2))
BESIDE = (
    ((3, 0), 0, (-1, 0)),
    ((0, 3), 0, (0, -1)),
    ((1, 3), 1, (0, -1)),
    ((0, 1), 2, (-1, 0)),
    ((2, 0), 3, (0, -1)),
    ((2, 3), 4, (0, 1)),
    ((1, 2), 4, (-1, 0)),
    ((0, 2), 5, (1, 0)),
    ((3, 3), 5, (0, 1)),
    ((3, 1), 5, (0, -1)),
)
SIGN = (1, -1)


def exchange_kernel(
    code, near_at, far_at, skel, blk, pts, interp, pot,
    fblk, tgt, stgt, sk, h01, h02, h03, h04, h05, h11, h12, h13, h14, h15, sb, rb, fb, ob,
    sc, rc, ss, rs, sf, rf,
):
    o, i = lax.axis_index("outer"), lax.axis_index("inner")
    y, c, x, z = o >> 1, o & 1, i >> 2, i & 3
    hub = ((blk.at[0], h01, h02, h03, h04, h05), (blk.at[1], h11, h12, h13, h14, h15))
    mine = (o * 16 + i) * 4

    def at_inner(dx, dz):
        return (((x + dx) & 3) << 2) | ((z + dz) & 3)

    def from_me(h, offset, sign=1):
        return at_inner(sign * SIGN[h] * offset[0], sign * SIGN[h] * offset[1])

    def along_y(d):
        return ((((y + d) & 3) << 1) | c, i)

    sibling = ((y << 1) | (1 - c), i)

    barrier = pltpu.get_barrier_semaphore()
    peers = [(o, at_inner(*d)) for d in ((1, 0), (-1, 0), (0, 1), (0, -1))] + [along_y(1), along_y(-1), sibling]
    for one in peers:
        pl.semaphore_signal(barrier, inc=1, device_id=one, device_id_type=MESH)
    pl.semaphore_wait(barrier, len(peers))

    def copy(src, dst, send, recv, to):
        return pltpu.make_async_remote_copy(
            src_ref=src, dst_ref=dst, send_sem=send, recv_sem=recv, device_id=to, device_id_type=MESH
        )

    def chain(h, k, leaf):
        (ax, az), (bx, bz) = CHAIN[k - 1], CHAIN[k]
        to = (o, from_me(h, (bx - ax, bz - az)))
        return copy(hub[h][k - 1].at[leaf], hub[h][k].at[leaf], sc.at[h, k - 1, leaf], rc.at[h, k - 1, leaf], to)

    def beside(h, n):
        return copy(sb.at[h, n], rb.at[h, n], ss.at[h, n], rs.at[h, n], (o, from_me(h, BESIDE[n][2])))

    def fbuf(dy, dc, lo=0, n=4):
        return fb.at[pl.ds((dy * 2 + dc - 1) * 4 + lo, n)]

    far_copies = {
        "up": copy(fblk, fbuf(1, 0), sf.at[0], rf.at[0], along_y(1)),
        "down": copy(fblk, fbuf(3, 0), sf.at[1], rf.at[1], along_y(-1)),
        "own": copy(fblk, fbuf(0, 1), sf.at[2], rf.at[2], sibling),
        "up2": copy(fbuf(1, 0, 0, 2), fbuf(2, 0, 0, 2), sf.at[3], rf.at[3], along_y(1)),
        "down2": copy(fbuf(3, 0, 2, 2), fbuf(2, 0, 2, 2), sf.at[4], rf.at[4], along_y(-1)),
        "side1": copy(fbuf(1, 0), fbuf(1, 1), sf.at[5], rf.at[5], sibling),
        "side3": copy(fbuf(3, 0), fbuf(3, 1), sf.at[6], rf.at[6], sibling),
        "side2": copy(fbuf(2, 0), fbuf(2, 1), sf.at[7], rf.at[7], sibling),
    }

    def wanted(dest, src, j):
        return code[src * 2 + j, (o * 16 + dest) * 4]

    def choose(n):
        offset, k, way = BESIDE[n]
        for h in range(2):
            src, dest = from_me(h, CHAIN[k], -1), from_me(h, way)
            for j in range(2):
                leaf = wanted(dest, src, j) & 3
                sb[h, n, j] = blk[h, leaf] if k == 0 else hub[h][k][leaf]
            beside(h, n).start()

    def serve(k, leaf):
        for h in range(2):
            chain(h, k, leaf).wait_recv()
            if k < 5:
                chain(h, k + 1, leaf).start()

    def add_tile(h, offset, j, load):
        src = from_me(h, offset, -1)
        v = wanted(i, src, j)
        at = (((SIGN[h] * offset[0]) % 4) * 4 + (SIGN[h] * offset[1]) % 4) * 2 + j
        ob[at] += tile(tgt[(v >> 2) & 3], source_operand(load(v & 3), (v >> 4).astype(F32)))

    def chain_tiles(k):
        for h in range(2):
            for j in range(2):
                add_tile(h, CHAIN[k], j, lambda leaf, h=h: hub[h][k][leaf])

    def beside_tiles(n):
        for h in range(2):
            beside(h, n).wait_recv()
            for j in range(2):
                add_tile(h, BESIDE[n][0], j, lambda leaf, h=h, j=j: rb[h, n, j])

    def halves(g):
        return [pl.ds(h * 1024 + g * HALF, HALF) for h in range(2)]

    def prepare(g):
        def pick(b, carry):
            at = [skel[g, b * 16 + u] for u in range(16)]
            rows = [pts[pl.ds((q >> 8) * 1024 + g * HALF + (q & 255), 1), :] for q in at]
            for u in range(16):
                sk[pl.ds(b * 16 + u, 1), :] = rows[u]
            return carry

        lax.fori_loop(0, 16, pick, 0)
        skt = jnp.transpose(sk[...])
        fblk[g, HALF : HALF + 64, :] = skt[0:64, 0:128]
        fblk[g, HALF + 64 : BLK, :] = skt[0:64, 128:256]
        stgt[g] = target_operand(sk[:, 0:DIM])
        charges = jnp.zeros((HALF, RHS), F32)
        for h, rows in enumerate(halves(g)):
            tgt[g, h * HALF : (h + 1) * HALF, :] = target_operand(pts[rows, 0:DIM])
            weights = interp[g * LEAF + h * HALF : g * LEAF + (h + 1) * HALF, :]
            charges = charges + dot3(weights, blk[h, g, 0:HALF, :], ((0,), (0,)))
        fblk[g, 0:HALF, :] = charges

    def own_tiles(g):
        near = tile(tgt[g], source_operand(blk[0, g], None)) + tile(tgt[g], source_operand(blk[1, g], None))
        for h, rows in enumerate(halves(g)):
            pot[rows, :] = near[h * HALF : (h + 1) * HALF, :]

    def far_leaf(g):
        def one(k, q):
            return q + tile(stgt[g], source_operand(fb[far_at[k, mine + g]], None))

        q = lax.fori_loop(0, 8, one, jnp.zeros((HALF, 128), F32))
        more = dot3(interp[g * LEAF : (g + 1) * LEAF, :], q)
        for h, rows in enumerate(halves(g)):
            pot[rows, :] += more[h * HALF : (h + 1) * HALF, :]

    def zero(t, carry):
        ob[t] = jnp.zeros((LEAF, 128), F32)
        return carry

    for leaf in range(4):
        for h in range(2):
            chain(h, 1, leaf).start()
    choose(1)
    prepare(0)
    serve(1, 0)
    prepare(1)
    prepare(2)
    serve(1, 1)
    serve(2, 0)
    prepare(3)
    for name in ("up", "down", "own"):
        far_copies[name].start()
    lax.fori_loop(0, 32, zero, 0)
    serve(1, 2)
    serve(2, 1)
    own_tiles(0)
    own_tiles(1)
    serve(1, 3)
    serve(2, 2)
    choose(2)
    own_tiles(2)
    serve(2, 3)
    serve(3, 0)
    choose(3)
    own_tiles(3)
    serve(3, 1)
    serve(4, 0)
    chain_tiles(1)
    serve(3, 2)
    serve(4, 1)
    for name, more in (("up", ("up2", "side1")), ("down", ("down2", "side3")), ("own", ())):
        far_copies[name].wait_recv()
        for m in more:
            far_copies[m].start()
    chain_tiles(2)
    serve(3, 3)
    serve(4, 2)
    choose(4)
    beside_tiles(1)
    serve(4, 3)
    choose(0)
    serve(5, 0)
    choose(5)
    choose(6)
    for name in ("up2", "down2"):
        far_copies[name].wait_recv()
    far_copies["side2"].start()
    chain_tiles(3)
    serve(5, 1)
    chain_tiles(4)
    serve(5, 2)
    beside_tiles(2)
    serve(5, 3)
    for n in (7, 8, 9):
        choose(n)
    for name in ("side1", "side3", "side2"):
        far_copies[name].wait_recv()
    for g in range(4):
        far_leaf(g)
    chain_tiles(5)
    for n in (0, 3, 4, 6, 5, 8, 7, 9):
        beside_tiles(n)

    for g in range(4):
        at = [near_at[k, mine + g] for k in range(1, 8)]
        for h, rows in enumerate(halves(g)):
            total = pot[rows, :]
            for k in range(7):
                total = total + ob[at[k], h * HALF : (h + 1) * HALF, :]
            pot[rows, :] = total

    for h in range(2):
        for k in range(1, 6):
            for leaf in range(4):
                chain(h, k, leaf).wait_send()
        for n in range(10):
            beside(h, n).wait_send()
    for one in far_copies.values():
        one.wait_send()


def exchange(code, near_at, far_at, skel, blk, pts, interp):
    dma = pltpu.SemaphoreType.DMA
    return pl.pallas_call(
        exchange_kernel,
        out_shape=jax.ShapeDtypeStruct((ROWS, RHS), F32),
        in_specs=[sspec()] * 4 + [vspec()] * 3,
        out_specs=vspec(),
        scratch_shapes=[
            pltpu.VMEM((4, BLK, 128), F32),
            pltpu.VMEM((4, LEAF, 256), BF16),
            pltpu.VMEM((4, HALF, 256), BF16),
            pltpu.VMEM((HALF, 128), F32),
        ]
        + [pltpu.VMEM((4, BLK, 128), F32)] * 10
        + [
            pltpu.VMEM((2, 10, 2, BLK, 128), F32),
            pltpu.VMEM((2, 10, 2, BLK, 128), F32),
            pltpu.VMEM((28, BLK, 128), F32),
            pltpu.VMEM((32, LEAF, 128), F32),
            dma((2, 5, 4)),
            dma((2, 5, 4)),
            dma((2, 10)),
            dma((2, 10)),
            dma((8,)),
            dma((8,)),
        ],
        compiler_params=pltpu.CompilerParams(
            vmem_limit_bytes=VMEM_LIMIT, collective_id=0, has_side_effects=True
        ),
    )(code, near_at, far_at, skel, blk, pts, interp)


def back_kernel(pos, pot, dst, buf, send, recv):
    me = lax.axis_index("outer") * 16 + lax.axis_index("inner")
    greet_all()
    pl.semaphore_wait(pltpu.get_barrier_semaphore(), DEVS - 1)

    def choose(d):
        return [pot[pl.ds(pos[d, u], 1), :] for u in range(16)]

    def go(t, carry):
        to = peer(t)
        d = to[0] * 16 + to[1]
        for u, row in enumerate(choose(d)):
            buf[d, u : u + 1, :] = row
        pltpu.make_async_remote_copy(
            src_ref=buf.at[d], dst_ref=dst.at[me], send_sem=send, recv_sem=recv, device_id=to, device_id_type=MESH
        ).start()
        return carry

    lax.fori_loop(1, DEVS, go, 0)
    for u, row in enumerate(choose(me)):
        dst[me, u : u + 1, :] = row
    most = pl.ds(0, DEVS - 1)
    whole = pltpu.make_async_remote_copy(
        src_ref=buf.at[most], dst_ref=dst.at[most], send_sem=send, recv_sem=recv,
        device_id=peer(1), device_id_type=MESH,
    )
    whole.wait_recv()
    whole.wait_send()


def rows_back(pos, pot):
    dma = pltpu.SemaphoreType.DMA
    shape = (DEVS, 16, RHS)
    return pl.pallas_call(
        back_kernel,
        out_shape=jax.ShapeDtypeStruct(shape, F32),
        in_specs=[sspec(), vspec()],
        out_specs=vspec(),
        scratch_shapes=[pltpu.VMEM(shape, F32), dma, dma],
        compiler_params=pltpu.CompilerParams(vmem_limit_bytes=VMEM_LIMIT, collective_id=2, has_side_effects=True),
    )(pos, pot).reshape(ROWS, RHS)


def spread_kernel(sort, src, dst):
    def body(b, carry):
        first = pl.multiple_of(b * 16, 16)
        to = [sort[b, u] for u in range(16)]
        rows = [src[pl.ds(first + u, 1), :] for u in range(16)]
        for u in range(16):
            dst[pl.ds(to[u], 1), :] = rows[u]
        return carry

    lax.fori_loop(0, DEVS, body, 0)


def spread_rows(sort, src):
    return pl.pallas_call(
        spread_kernel,
        out_shape=jax.ShapeDtypeStruct((ROWS, RHS), F32),
        in_specs=[sspec(), vspec()],
        out_specs=vspec(),
        compiler_params=pltpu.CompilerParams(vmem_limit_bytes=VMEM_LIMIT),
    )(sort, src)


def shards(points, charges, interp, order, near, far, skel):
    sort, posmat, code, near_at, far_at = make_plan(order, near, far)
    got, pos = rows_out(sort, posmat, points, charges)
    blk, pts = place_rows(pos, got)
    pot = exchange(code, near_at, far_at, skel, blk, pts, interp)
    return spread_rows(sort, rows_back(pos, pot))


def solution(mesh):
    rows = P(("outer", "inner"), None)
    return jax.shard_map(
        shards,
        mesh=mesh,
        in_specs=(rows, rows, rows, P(("outer", "inner")), P(), P(), rows),
        out_specs=rows,
        check_vma=False,
    )
```

```python
import functools
import math

import jax
import jax.numpy as jnp
from jax import lax
from jax.experimental import pallas as pl
from jax.experimental.pallas import tpu as pltpu
from jax.sharding import PartitionSpec as P

F32, BF16, I32 = jnp.float32, jnp.bfloat16, jnp.int32
MESH = pl.DeviceIdType.MESH
VMEM_LIMIT = 60 * 1024 * 1024

ROWS = 2048
DEVS = 128
LEAF = 512
HALF = 256
DIM = 64
RHS = 128
BLK = HALF + 128
SCALE = math.log2(math.e) * 4.0 / DIM


def vspec():
    return pl.BlockSpec(memory_space=pltpu.VMEM)


def sspec():
    return pl.BlockSpec(memory_space=pltpu.SMEM)


def dot(a, b, contract=((1,), (0,))):
    return lax.dot_general(a, b, (contract, ((), ())), preferred_element_type=F32)


def hi_lo(v):
    hi = v.astype(BF16)
    return hi, (v - hi.astype(F32)).astype(BF16)


def dot3(a, b, contract=((1,), (0,))):
    ah, al = hi_lo(a)
    bh, bl = hi_lo(b)
    return dot(ah, bh, contract) + dot(ah, bl, contract) + dot(al, bh, contract)


def three(v):
    hi = v.astype(BF16).astype(F32)
    rest = v - hi
    mid = rest.astype(BF16).astype(F32)
    return hi, mid, rest - mid


def widened(v):
    return jnp.concatenate([v, jnp.zeros((128, 112), F32)], axis=1)


def slots_first(v):
    return jnp.transpose(widened(v))[0:16, :].astype(I32) & (ROWS - 1)


def plan(order_ref, near_ref, far_ref, rank_ref, sort_ref, posmat_ref, code_ref, near_at_ref, far_at_ref):
    sub = lax.broadcasted_iota(I32, (128, 128), 0)
    lane = lax.broadcasted_iota(I32, (128, 128), 1)
    before = (sub < lane).astype(F32).astype(BF16)
    ones = jnp.ones((128, 128), BF16)
    base = jnp.zeros((128, 128), F32)
    both = jnp.zeros((512, 16), F32)
    for r in range(ROWS // 128):
        order = order_ref[r : r + 1, :]
        owner = order >> 11
        hit = (sub == owner).astype(F32)
        hit16 = hit.astype(BF16)
        seen = dot(hit16, before) + base
        base = base + dot(hit16, ones)
        nth = jnp.sum(hit * seen, axis=0, keepdims=True).astype(I32)
        rank_ref[r : r + 1, :] = (owner * 16 + nth) & (ROWS - 1)
        pos = ((order >> 8) & 1) * 1024 + ((order >> 9) & 3) * HALF + (order & 255)
        slot = (sub[0:16] == nth).astype(F32).astype(BF16)
        row = lane[0:1] + r * 128
        pieces = [(hit * v.astype(F32)).astype(BF16) for v in (pos >> 4, pos & 15, row >> 4, row & 15)]
        both = both + dot(jnp.concatenate(pieces, axis=0), slot, ((1,), (1,)))
    posmat_ref[...] = widened(16.0 * both[0:128] + both[128:256])
    sort_ref[...] = slots_first(16.0 * both[256:384] + both[384:512])

    o, i = lax.axis_index("outer"), lax.axis_index("inner")
    y, c, x, z = o >> 1, o & 1, i >> 2, i & 3
    entry = near_ref[...]
    row = lax.broadcasted_iota(I32, entry.shape, 0)
    g = lax.broadcasted_iota(I32, entry.shape, 1) & 3
    src = jnp.where(row == 0, -1, (entry >> 2) & 15)
    nth = jnp.zeros(entry.shape, I32)
    for back in range(4):
        other = src if back == 0 else pltpu.roll(src, back, axis=1)
        for k in range(1, 8):
            earlier = (row > k) if back == 0 else (g >= back)
            nth = nth + jnp.where((other[k : k + 1, :] == src) & earlier, 1, 0)
    place = src * 2 + nth
    mark = 16 + 4 * g + (entry & 3)
    want = lax.broadcasted_iota(I32, (32, entry.shape[1]), 0)
    code = jnp.zeros(want.shape, I32)
    for k in range(1, 8):
        code = code + jnp.where(want == place[k : k + 1, :], mark[k : k + 1, :], 0)
    n = code.shape[1]
    code = code + pltpu.roll(code, n - 1, axis=1)
    code_ref[...] = code + pltpu.roll(code, n - 2, axis=1)
    near_at_ref[...] = ((((x - (src >> 2)) & 3) * 4 + ((z - src) & 3)) * 2 + nth) & 31
    f = far_ref[...]
    fo = f >> 6
    device = jnp.maximum(((y - (fo >> 1)) & 3) * 2 + ((c + fo) & 1), 1)
    far_at_ref[...] = (device - 1) * 4 + (f & 3)


SENT = 25


def peer(t):
    o, i = lax.axis_index("outer"), lax.axis_index("inner")
    y, c, x, z = o >> 1, o & 1, i >> 2, i & 3
    a, b, e, other = t & 3, (t >> 2) & 3, (t >> 4) & 3, t >> 6
    return ((((y + a) & 3) << 1) | (c ^ other), (((x + a + b) & 3) << 2) | ((z + e + 3 * a) & 3))


def greet_all():
    def greet(t, carry):
        pl.semaphore_signal(pltpu.get_barrier_semaphore(), inc=1, device_id=peer(t), device_id_type=MESH)
        return carry

    lax.fori_loop(1, DEVS, greet, 0)


def target_operand(x):
    n = x.shape[0]
    hi, lo = hi_lo(x * (2.0 * SCALE))
    norm = jnp.sum(x * x, axis=1, keepdims=True) * (-SCALE)
    n0, n1, n2 = three(norm)
    lane = lax.broadcasted_iota(I32, (n, DIM), 1)
    tail = jnp.where(
        lane == 0, n0, jnp.where(lane == 1, n1, jnp.where(lane == 2, n2, jnp.where(lane < 6, 1.0, 0.0)))
    )
    return jnp.concatenate([hi, hi, lo, tail.astype(BF16)], axis=1)


def source_operand(block, scale):
    xt = jnp.concatenate([block[HALF : HALF + 64, :], block[HALF + 64 : BLK, :]], axis=1)
    hi, lo = hi_lo(xt)
    norm = jnp.sum(xt * xt, axis=0, keepdims=True) * (-SCALE)
    n0, n1, n2 = three(norm)
    row = lax.broadcasted_iota(I32, (16, HALF), 0)
    tail = jnp.where(
        row < 3, 1.0, jnp.where(row == 3, n0, jnp.where(row == 4, n1, jnp.where(row == 5, n2, 0.0)))
    )
    right = jnp.concatenate([hi, lo, hi, tail.astype(BF16), jnp.zeros((48, HALF), BF16)], axis=0)
    chg = block[0:HALF, :]
    if scale is not None:
        chg = chg * scale
    ch, cl = hi_lo(chg)
    return right, jnp.concatenate([ch, cl], axis=1)


def tile(target, operand):
    right, both = operand
    n = target.shape[0]
    g = jnp.exp2(dot(target, right))
    gh, gl = hi_lo(g)
    wide = dot(jnp.concatenate([gh, gl], axis=0), both)
    return wide[:n, 0:128] + (wide[:n, 128:256] + wide[n:, 0:128])


CHAIN = ((0, 0), (1, 0), (1, 1), (2, 1), (2, 2), (3, 2))
BESIDE = (
    ((3, 0), 0, (-1, 0)),
    ((0, 3), 0, (0, -1)),
    ((1, 3), 1, (0, -1)),
    ((0, 1), 2, (-1, 0)),
    ((2, 0), 3, (0, -1)),
    ((2, 3), 4, (0, 1)),
    ((1, 2), 4, (-1, 0)),
    ((0, 2), 5, (1, 0)),
    ((3, 3), 5, (0, 1)),
    ((3, 1), 5, (0, -1)),
)
SIGN = (1, -1)


def exchange_kernel(
    order, near, far, skel, pts_in, chg_in, interp, out,
    rank_v, sort_v, posmat, code_v, near_v, far_v, pos_v, inv_v, rank, sort, code, near_at, far_at, pos, inv, st,
    wide, packed, got, so, ro, blk, pts, pot, leaving, landed, fblk, tgt, stgt, sk, h01, h02, h03, h04, h05, h11, h12, h13, h14, h15, sb, rb, fb, ob,
    sc, rc, ss, rs, sf, rf, sl, rl,
):
    o, i = lax.axis_index("outer"), lax.axis_index("inner")
    y, c, x, z = o >> 1, o & 1, i >> 2, i & 3
    hub = ((blk.at[0], h01, h02, h03, h04, h05), (blk.at[1], h11, h12, h13, h14, h15))
    mine = (o * 16 + i) * 4

    def at_inner(dx, dz):
        return (((x + dx) & 3) << 2) | ((z + dz) & 3)

    def from_me(h, offset, sign=1):
        return at_inner(sign * SIGN[h] * offset[0], sign * SIGN[h] * offset[1])

    def along_y(d):
        return ((((y + d) & 3) << 1) | c, i)

    sibling = ((y << 1) | (1 - c), i)

    me = o * 16 + i
    greet_all()
    plan(order, near, far, rank_v, sort_v, posmat, code_v, near_v, far_v)

    def to_scalars(k, src, dst):
        return pltpu.make_async_copy(src, dst, st.at[k])

    moves = [to_scalars(0, sort_v, sort), to_scalars(1, rank_v, rank), to_scalars(2, code_v, code)]
    moves += [to_scalars(3, near_v, near_at), to_scalars(4, far_v, far_at)]
    for one in moves:
        one.start()
    for r in range(ROWS // 128):
        cols = pts_in[:, r * 128 : (r + 1) * 128]
        wide[r * 128 : (r + 1) * 128, :] = jnp.transpose(jnp.concatenate([cols, cols], axis=0))
    for one in moves:
        one.wait()
    left = lax.broadcasted_iota(I32, (1, 128), 1) < DIM

    def pack(ref, d):
        at = [sort[u, d] for u in range(16)]
        c16 = [chg_in[pl.ds(n, 1), :] for n in at]
        p16 = [wide[pl.ds(n, 1), :] for n in at]
        for u in range(16):
            ref[d, u : u + 1, :] = c16[u]
        for u in range(8):
            ref[d, 16 + u : 17 + u, :] = jnp.where(left, p16[u], p16[u + 8])
        ref[d, 24:25, :] = posmat[pl.ds(d, 1), :]

    pack(got, me)
    pl.semaphore_wait(pltpu.get_barrier_semaphore(), DEVS - 1)

    def copy(src, dst, send, recv, to):
        return pltpu.make_async_remote_copy(
            src_ref=src, dst_ref=dst, send_sem=send, recv_sem=recv, device_id=to, device_id_type=MESH
        )

    sent_rows = pl.ds(0, SENT)
    most = pl.ds(0, DEVS - 1)

    def send_out(t, carry):
        to = peer(t)
        d = to[0] * 16 + to[1]
        pack(packed, d)
        copy(packed.at[d, sent_rows], got.at[me, sent_rows], so, ro, to).start()
        return carry

    lax.fori_loop(1, DEVS, send_out, 0)
    all_out = copy(packed.at[most, sent_rows], got.at[most, sent_rows], so, ro, peer(1))
    all_out.wait_recv()

    arrived = jnp.transpose(got[:, 24, :])[0:16, :].astype(I32) & (ROWS - 1)
    pos_v[...] = arrived
    sub = lax.broadcasted_iota(I32, (128, 128), 0)
    lane = lax.broadcasted_iota(I32, (128, 128), 1).astype(F32)
    both = jnp.zeros((256, 16), F32)
    for u in range(16):
        p = arrived[u : u + 1, :]
        hit = (sub == (p >> 4)).astype(F32)
        low = (sub[0:16] == (p & 15)).astype(F32).astype(BF16)
        pieces = jnp.concatenate([(hit * lane).astype(BF16), (hit * float(u)).astype(BF16)], axis=0)
        both = both + dot(pieces, low, ((1,), (1,)))
    inv_v[...] = slots_first(16.0 * both[0:128] + both[128:256])
    moves = [to_scalars(5, pos_v, pos), to_scalars(6, inv_v, inv)]
    for one in moves:
        one.start()

    def unpack(d, carry):
        rows = got[d, 16:24, :]
        wide[pl.ds(pl.multiple_of(d * 16, 16), 8), :] = rows
        wide[pl.ds(pl.multiple_of(d * 16 + 8, 8), 8), :] = pltpu.roll(rows, DIM, axis=1)
        return carry

    lax.fori_loop(0, DEVS, unpack, 0)
    for one in moves:
        one.wait()

    def place(h, g):
        def some(b, carry):
            at = [inv[u, h * 64 + g * 16 + b] for u in range(16)]
            c16 = [got[n >> 4, pl.ds(n & 15, 1), :] for n in at]
            p16 = [wide[pl.ds(n, 1), :] for n in at]
            first = pl.multiple_of(b * 16, 16)
            for u in range(16):
                blk[h, g, pl.ds(first + u, 1), :] = c16[u]
                pts[pl.ds(h * 1024 + g * HALF + first + u, 1), :] = p16[u]
            return carry

        lax.fori_loop(0, 16, some, 0)
        xt = jnp.transpose(pts[h * 1024 + g * HALF : h * 1024 + (g + 1) * HALF, :])
        blk[h, g, HALF : HALF + 64, :] = xt[0:64, 0:128]
        blk[h, g, HALF + 64 : BLK, :] = xt[0:64, 128:256]

    def chain(h, k, leaf):
        (ax, az), (bx, bz) = CHAIN[k - 1], CHAIN[k]
        to = (o, from_me(h, (bx - ax, bz - az)))
        return copy(hub[h][k - 1].at[leaf], hub[h][k].at[leaf], sc.at[h, k - 1, leaf], rc.at[h, k - 1, leaf], to)

    def beside(h, n):
        return copy(sb.at[h, n], rb.at[h, n], ss.at[h, n], rs.at[h, n], (o, from_me(h, BESIDE[n][2])))

    def fbuf(dy, dc, lo=0, n=4):
        return fb.at[pl.ds((dy * 2 + dc - 1) * 4 + lo, n)]

    far_copies = {
        "up": copy(fblk, fbuf(1, 0), sf.at[0], rf.at[0], along_y(1)),
        "down": copy(fblk, fbuf(3, 0), sf.at[1], rf.at[1], along_y(-1)),
        "own": copy(fblk, fbuf(0, 1), sf.at[2], rf.at[2], sibling),
        "up2": copy(fbuf(1, 0, 0, 2), fbuf(2, 0, 0, 2), sf.at[3], rf.at[3], along_y(1)),
        "down2": copy(fbuf(3, 0, 2, 2), fbuf(2, 0, 2, 2), sf.at[4], rf.at[4], along_y(-1)),
        "side1": copy(fbuf(1, 0), fbuf(1, 1), sf.at[5], rf.at[5], sibling),
        "side3": copy(fbuf(3, 0), fbuf(3, 1), sf.at[6], rf.at[6], sibling),
        "side2": copy(fbuf(2, 0), fbuf(2, 1), sf.at[7], rf.at[7], sibling),
    }

    def wanted(dest, src, j):
        return code[src * 2 + j, (o * 16 + dest) * 4]

    def choose(n):
        offset, k, way = BESIDE[n]
        for h in range(2):
            src, dest = from_me(h, CHAIN[k], -1), from_me(h, way)
            for j in range(2):
                leaf = wanted(dest, src, j) & 3
                sb[h, n, j] = blk[h, leaf] if k == 0 else hub[h][k][leaf]
            beside(h, n).start()

    def serve(k, leaf):
        for h in range(2):
            chain(h, k, leaf).wait_recv()
            if k < 5:
                chain(h, k + 1, leaf).start()

    def add_tile(h, offset, j, load):
        src = from_me(h, offset, -1)
        v = wanted(i, src, j)
        at = (((SIGN[h] * offset[0]) % 4) * 4 + (SIGN[h] * offset[1]) % 4) * 2 + j
        ob[at] += tile(tgt[(v >> 2) & 3], source_operand(load(v & 3), (v >> 4).astype(F32)))

    def chain_tiles(k):
        for h in range(2):
            for j in range(2):
                add_tile(h, CHAIN[k], j, lambda leaf, h=h: hub[h][k][leaf])

    def beside_tiles(n):
        for h in range(2):
            beside(h, n).wait_recv()
            for j in range(2):
                add_tile(h, BESIDE[n][0], j, lambda leaf, h=h, j=j: rb[h, n, j])

    def halves(g):
        return [pl.ds(h * 1024 + g * HALF, HALF) for h in range(2)]

    def prepare(g):
        def pick(b, carry):
            at = [skel[g, b * 16 + u] for u in range(16)]
            rows = [pts[pl.ds((q >> 8) * 1024 + g * HALF + (q & 255), 1), :] for q in at]
            for u in range(16):
                sk[pl.ds(b * 16 + u, 1), :] = rows[u]
            return carry

        lax.fori_loop(0, 16, pick, 0)
        skt = jnp.transpose(sk[...])
        fblk[g, HALF : HALF + 64, :] = skt[0:64, 0:128]
        fblk[g, HALF + 64 : BLK, :] = skt[0:64, 128:256]
        stgt[g] = target_operand(sk[:, 0:DIM])
        charges = jnp.zeros((HALF, RHS), F32)
        for h, rows in enumerate(halves(g)):
            tgt[g, h * HALF : (h + 1) * HALF, :] = target_operand(pts[rows, 0:DIM])
            weights = interp[g * LEAF + h * HALF : g * LEAF + (h + 1) * HALF, :]
            charges = charges + dot3(weights, blk[h, g, 0:HALF, :], ((0,), (0,)))
        fblk[g, 0:HALF, :] = charges

    def own_tiles(g):
        near = tile(tgt[g], source_operand(blk[0, g], None)) + tile(tgt[g], source_operand(blk[1, g], None))
        for h, rows in enumerate(halves(g)):
            pot[rows, :] = near[h * HALF : (h + 1) * HALF, :]

    def far_leaf(g):
        def one(k, q):
            return q + tile(stgt[g], source_operand(fb[far_at[k, mine + g]], None))

        q = lax.fori_loop(0, 8, one, jnp.zeros((HALF, 128), F32))
        more = dot3(interp[g * LEAF : (g + 1) * LEAF, :], q)
        for h, rows in enumerate(halves(g)):
            pot[rows, :] += more[h * HALF : (h + 1) * HALF, :]

    def zero(t, carry):
        ob[t] = jnp.zeros((LEAF, 128), F32)
        return carry

    for leaf in range(4):
        for h in range(2):
            place(h, leaf)
            chain(h, 1, leaf).start()
    choose(1)
    prepare(0)
    serve(1, 0)
    prepare(1)
    prepare(2)
    serve(1, 1)
    serve(2, 0)
    prepare(3)
    for name in ("up", "down", "own"):
        far_copies[name].start()
    lax.fori_loop(0, 32, zero, 0)
    serve(1, 2)
    serve(2, 1)
    own_tiles(0)
    own_tiles(1)
    serve(1, 3)
    serve(2, 2)
    choose(2)
    own_tiles(2)
    serve(2, 3)
    serve(3, 0)
    choose(3)
    own_tiles(3)
    serve(3, 1)
    serve(4, 0)
    chain_tiles(1)
    serve(3, 2)
    serve(4, 1)
    for name, more in (("up", ("up2", "side1")), ("down", ("down2", "side3")), ("own", ())):
        far_copies[name].wait_recv()
        for m in more:
            far_copies[m].start()
    chain_tiles(2)
    serve(3, 3)
    serve(4, 2)
    choose(4)
    beside_tiles(1)
    serve(4, 3)
    choose(0)
    serve(5, 0)
    choose(5)
    choose(6)
    for name in ("up2", "down2"):
        far_copies[name].wait_recv()
    far_copies["side2"].start()
    chain_tiles(3)
    serve(5, 1)
    chain_tiles(4)
    serve(5, 2)
    beside_tiles(2)
    serve(5, 3)
    for n in (7, 8, 9):
        choose(n)
    for name in ("side1", "side3", "side2"):
        far_copies[name].wait_recv()
    for g in range(4):
        far_leaf(g)
    chain_tiles(5)
    for n in (0, 3, 4, 6, 5, 8, 7, 9):
        beside_tiles(n)

    for g in range(4):
        at = [near_at[k, mine + g] for k in range(1, 8)]
        for h, rows in enumerate(halves(g)):
            total = pot[rows, :]
            for k in range(7):
                total = total + ob[at[k], h * HALF : (h + 1) * HALF, :]
            pot[rows, :] = total

    def gather(ref, at, d):
        rows = [pot[pl.ds(pos[u, d], 1), :] for u in range(16)]
        for u in range(16):
            ref[at, u : u + 1, :] = rows[u]

    def send_back(t, carry):
        to = peer(t)
        d = to[0] * 16 + to[1]
        gather(leaving, d, d)
        copy(leaving.at[d], landed.at[me], sl, rl, to).start()
        return carry

    lax.fori_loop(1, DEVS, send_back, 0)
    gather(landed, me, me)
    for h in range(2):
        for k in range(1, 6):
            for leaf in range(4):
                chain(h, k, leaf).wait_send()
        for n in range(10):
            beside(h, n).wait_send()
    for one in far_copies.values():
        one.wait_send()
    whole = copy(leaving.at[most], landed.at[most], sl, rl, peer(1))
    whole.wait_recv()

    def spread(b, carry):
        first = pl.multiple_of(b * 16, 16)
        at = [rank[b >> 3, (b & 7) * 16 + u] for u in range(16)]
        rows = [landed[n >> 4, pl.ds(n & 15, 1), :] for n in at]
        for u in range(16):
            out[pl.ds(first + u, 1), :] = rows[u]
        return carry

    lax.fori_loop(0, ROWS // 16, spread, 0)
    whole.wait_send()
    all_out.wait_send()


def exchange(order, near, far, skel, points, charges, interp):
    dma = pltpu.SemaphoreType.DMA
    return pl.pallas_call(
        exchange_kernel,
        out_shape=jax.ShapeDtypeStruct((ROWS, RHS), F32),
        in_specs=[vspec()] * 3 + [sspec()] + [vspec()] * 3,
        out_specs=vspec(),
        scratch_shapes=[
            pltpu.VMEM((16, 128), I32),
            pltpu.VMEM((16, 128), I32),
            pltpu.VMEM((DEVS, 128), F32),
            pltpu.VMEM((32, near.shape[0]), I32),
            pltpu.VMEM((8, near.shape[0]), I32),
            pltpu.VMEM((8, near.shape[0]), I32),
            pltpu.VMEM((16, 128), I32),
            pltpu.VMEM((16, 128), I32),
            pltpu.SMEM((16, 128), I32),
            pltpu.SMEM((16, 128), I32),
            pltpu.SMEM((32, near.shape[0]), I32),
            pltpu.SMEM((8, near.shape[0]), I32),
            pltpu.SMEM((8, near.shape[0]), I32),
            pltpu.SMEM((16, 128), I32),
            pltpu.SMEM((16, 128), I32),
            dma((7,)),
            pltpu.VMEM((ROWS, 128), F32),
            pltpu.VMEM((DEVS, 32, 128), F32),
            pltpu.VMEM((DEVS, 32, 128), F32),
            dma,
            dma,
            pltpu.VMEM((2, 4, BLK, 128), F32),
            pltpu.VMEM((ROWS, 128), F32),
            pltpu.VMEM((ROWS, RHS), F32),
            pltpu.VMEM((DEVS, 16, RHS), F32),
            pltpu.VMEM((DEVS, 16, RHS), F32),
            pltpu.VMEM((4, BLK, 128), F32),
            pltpu.VMEM((4, LEAF, 256), BF16),
            pltpu.VMEM((4, HALF, 256), BF16),
            pltpu.VMEM((HALF, 128), F32),
        ]
        + [pltpu.VMEM((4, BLK, 128), F32)] * 10
        + [
            pltpu.VMEM((2, 10, 2, BLK, 128), F32),
            pltpu.VMEM((2, 10, 2, BLK, 128), F32),
            pltpu.VMEM((28, BLK, 128), F32),
            pltpu.VMEM((32, LEAF, 128), F32),
            dma((2, 5, 4)),
            dma((2, 5, 4)),
            dma((2, 10)),
            dma((2, 10)),
            dma((8,)),
            dma((8,)),
            dma,
            dma,
        ],
        compiler_params=pltpu.CompilerParams(
            vmem_limit_bytes=VMEM_LIMIT, collective_id=0, has_side_effects=True
        ),
    )(order.reshape(16, 128), near.T, far.T, skel, points.T, charges, interp)


def shards(points, charges, interp, order, near, far, skel):
    return exchange(order, near, far, skel, points, charges, interp)


def solution(mesh):
    rows = P(("outer", "inner"), None)
    return jax.shard_map(
        shards,
        mesh=mesh,
        in_specs=(rows, rows, rows, P(("outer", "inner")), P(), P(), rows),
        out_specs=rows,
        check_vma=False,
    )
```

```python
import functools
import math

import jax
import jax.numpy as jnp
from jax import lax
from jax.experimental import pallas as pl
from jax.experimental.pallas import tpu as pltpu
from jax.sharding import PartitionSpec as P

F32, BF16, I32 = jnp.float32, jnp.bfloat16, jnp.int32
MESH = pl.DeviceIdType.MESH
VMEM_LIMIT = 60 * 1024 * 1024

ROWS = 2048
DEVS = 128
LEAF = 512
HALF = 256
DIM = 64
RHS = 128
BLK = HALF + 128
SCALE = math.log2(math.e) * 4.0 / DIM


def vspec():
    return pl.BlockSpec(memory_space=pltpu.VMEM)


def sspec():
    return pl.BlockSpec(memory_space=pltpu.SMEM)


def dot(a, b, contract=((1,), (0,))):
    return lax.dot_general(a, b, (contract, ((), ())), preferred_element_type=F32)


def hi_lo(v):
    hi = v.astype(BF16)
    return hi, (v - hi.astype(F32)).astype(BF16)


def dot3(a, b, contract=((1,), (0,))):
    ah, al = hi_lo(a)
    bh, bl = hi_lo(b)
    return dot(ah, bh, contract) + dot(ah, bl, contract) + dot(al, bh, contract)


def three(v):
    hi = v.astype(BF16).astype(F32)
    rest = v - hi
    mid = rest.astype(BF16).astype(F32)
    return hi, mid, rest - mid


def widened(v):
    return jnp.concatenate([v, jnp.zeros((128, 112), F32)], axis=1)


def slots_first(v):
    return jnp.transpose(widened(v))[0:16, :].astype(I32) & (ROWS - 1)


def plan(order_ref, near_ref, far_ref, rank_ref, sort_ref, posmat_ref, code_ref, near_at_ref, far_at_ref):
    sub = lax.broadcasted_iota(I32, (128, 128), 0)
    lane = lax.broadcasted_iota(I32, (128, 128), 1)
    before = (sub < lane).astype(F32).astype(BF16)
    ones = jnp.ones((128, 128), BF16)
    base = jnp.zeros((128, 128), F32)
    both = jnp.zeros((512, 16), F32)
    for r in range(ROWS // 128):
        order = order_ref[r : r + 1, :]
        owner = order >> 11
        hit = (sub == owner).astype(F32)
        hit16 = hit.astype(BF16)
        seen = dot(hit16, before) + base
        base = base + dot(hit16, ones)
        nth = jnp.sum(hit * seen, axis=0, keepdims=True).astype(I32)
        rank_ref[r : r + 1, :] = (owner * 16 + nth) & (ROWS - 1)
        pos = ((order >> 8) & 1) * 1024 + ((order >> 9) & 3) * HALF + (order & 255)
        slot = (sub[0:16] == nth).astype(F32).astype(BF16)
        row = lane[0:1] + r * 128
        pieces = [(hit * v.astype(F32)).astype(BF16) for v in (pos >> 4, pos & 15, row >> 4, row & 15)]
        both = both + dot(jnp.concatenate(pieces, axis=0), slot, ((1,), (1,)))
    posmat_ref[...] = widened(16.0 * both[0:128] + both[128:256])
    sort_ref[...] = slots_first(16.0 * both[256:384] + both[384:512])

    o, i = lax.axis_index("outer"), lax.axis_index("inner")
    y, c, x, z = o >> 1, o & 1, i >> 2, i & 3
    entry = near_ref[...]
    row = lax.broadcasted_iota(I32, entry.shape, 0)
    g = lax.broadcasted_iota(I32, entry.shape, 1) & 3
    src = jnp.where(row == 0, -1, (entry >> 2) & 15)
    nth = jnp.zeros(entry.shape, I32)
    for back in range(4):
        other = src if back == 0 else pltpu.roll(src, back, axis=1)
        for k in range(1, 8):
            earlier = (row > k) if back == 0 else (g >= back)
            nth = nth + jnp.where((other[k : k + 1, :] == src) & earlier, 1, 0)
    place = src * 2 + nth
    mark = 16 + 4 * g + (entry & 3)
    want = lax.broadcasted_iota(I32, (32, entry.shape[1]), 0)
    code = jnp.zeros(want.shape, I32)
    for k in range(1, 8):
        code = code + jnp.where(want == place[k : k + 1, :], mark[k : k + 1, :], 0)
    n = code.shape[1]
    code = code + pltpu.roll(code, n - 1, axis=1)
    code_ref[...] = code + pltpu.roll(code, n - 2, axis=1)
    near_at_ref[...] = ((((x - (src >> 2)) & 3) * 4 + ((z - src) & 3)) * 2 + nth) & 31
    f = far_ref[...]
    fo = f >> 6
    device = jnp.maximum(((y - (fo >> 1)) & 3) * 2 + ((c + fo) & 1), 1)
    far_at_ref[...] = (device - 1) * 4 + (f & 3)


SENT = 25


def peer(t):
    o, i = lax.axis_index("outer"), lax.axis_index("inner")
    y, c, x, z = o >> 1, o & 1, i >> 2, i & 3
    a, b, e, other = t & 3, (t >> 2) & 3, (t >> 4) & 3, t >> 6
    return ((((y + a) & 3) << 1) | (c ^ other), (((x + a + b) & 3) << 2) | ((z + e + 3 * a) & 3))


def greet_all():
    def greet(t, carry):
        pl.semaphore_signal(pltpu.get_barrier_semaphore(), inc=1, device_id=peer(t), device_id_type=MESH)
        return carry

    lax.fori_loop(1, DEVS, greet, 0)


def target_operand(x):
    n = x.shape[0]
    hi, lo = hi_lo(x * (2.0 * SCALE))
    norm = jnp.sum(x * x, axis=1, keepdims=True) * (-SCALE)
    n0, n1, n2 = three(norm)
    lane = lax.broadcasted_iota(I32, (n, DIM), 1)
    tail = jnp.where(
        lane == 0, n0, jnp.where(lane == 1, n1, jnp.where(lane == 2, n2, jnp.where(lane < 6, 1.0, 0.0)))
    )
    return jnp.concatenate([hi, hi, lo, tail.astype(BF16)], axis=1)


def source_operand(block, scale):
    xt = jnp.concatenate([block[HALF : HALF + 64, :], block[HALF + 64 : BLK, :]], axis=1)
    hi, lo = hi_lo(xt)
    norm = jnp.sum(xt * xt, axis=0, keepdims=True) * (-SCALE)
    n0, n1, n2 = three(norm)
    row = lax.broadcasted_iota(I32, (16, HALF), 0)
    tail = jnp.where(
        row < 3, 1.0, jnp.where(row == 3, n0, jnp.where(row == 4, n1, jnp.where(row == 5, n2, 0.0)))
    )
    right = jnp.concatenate([hi, lo, hi, tail.astype(BF16), jnp.zeros((48, HALF), BF16)], axis=0)
    chg = block[0:HALF, :]
    if scale is not None:
        chg = chg * scale
    ch, cl = hi_lo(chg)
    return right, jnp.concatenate([ch, cl], axis=1)


def tile(target, operand):
    right, both = operand
    n = target.shape[0]
    g = jnp.exp2(dot(target, right))
    gh, gl = hi_lo(g)
    wide = dot(jnp.concatenate([gh, gl], axis=0), both)
    return wide[:n, 0:128] + (wide[:n, 128:256] + wide[n:, 0:128])


CHAIN = ((0, 0), (1, 0), (1, 1), (2, 1), (2, 2), (3, 2))
BESIDE = (
    ((3, 0), 0, (-1, 0)),
    ((0, 3), 0, (0, -1)),
    ((1, 3), 1, (0, -1)),
    ((0, 1), 2, (-1, 0)),
    ((2, 0), 3, (0, -1)),
    ((2, 3), 4, (0, 1)),
    ((1, 2), 4, (-1, 0)),
    ((0, 2), 5, (1, 0)),
    ((3, 3), 5, (0, 1)),
    ((3, 1), 5, (0, -1)),
)
SIGN = (1, -1)


def exchange_kernel(
    order, near, far, skel, pts_hbm, chg_hbm, interp_hbm, out_hbm,
    pts_in, chg_in, interp, out, sh,
    rank_v, sort_v, posmat, code_v, near_v, far_v, pos_v, inv_v, rank, sort, code, near_at, far_at, pos, inv, st,
    wide, packed, got, so, ro, blk, pts, pot, leaving, landed, fblk, tgt, stgt, sk, h01, h02, h03, h04, h05, h11, h12, h13, h14, h15, sb, rb, fb, ob,
    sc, rc, ss, rs, sf, rf, sl, rl,
):
    o, i = lax.axis_index("outer"), lax.axis_index("inner")
    y, c, x, z = o >> 1, o & 1, i >> 2, i & 3
    hub = ((blk.at[0], h01, h02, h03, h04, h05), (blk.at[1], h11, h12, h13, h14, h15))
    mine = (o * 16 + i) * 4

    def at_inner(dx, dz):
        return (((x + dx) & 3) << 2) | ((z + dz) & 3)

    def from_me(h, offset, sign=1):
        return at_inner(sign * SIGN[h] * offset[0], sign * SIGN[h] * offset[1])

    def along_y(d):
        return ((((y + d) & 3) << 1) | c, i)

    sibling = ((y << 1) | (1 - c), i)

    me = o * 16 + i
    loads = [
        pltpu.make_async_copy(src, dst, sh.at[k])
        for k, (src, dst) in enumerate(((pts_hbm, pts_in), (chg_hbm, chg_in), (interp_hbm, interp)))
    ]
    for one in loads:
        one.start()
    greet_all()
    plan(order, near, far, rank_v, sort_v, posmat, code_v, near_v, far_v)

    def to_scalars(k, src, dst):
        return pltpu.make_async_copy(src, dst, st.at[k])

    moves = [to_scalars(0, sort_v, sort), to_scalars(1, rank_v, rank), to_scalars(2, code_v, code)]
    moves += [to_scalars(3, near_v, near_at), to_scalars(4, far_v, far_at)]
    for one in moves:
        one.start()
    loads[0].wait()
    for r in range(ROWS // 128):
        cols = pts_in[:, r * 128 : (r + 1) * 128]
        wide[r * 128 : (r + 1) * 128, :] = jnp.transpose(jnp.concatenate([cols, cols], axis=0))
    for one in moves:
        one.wait()
    left = lax.broadcasted_iota(I32, (1, 128), 1) < DIM

    def pack(ref, d):
        at = [sort[u, d] for u in range(16)]
        c16 = [chg_in[pl.ds(n, 1), :] for n in at]
        p16 = [wide[pl.ds(n, 1), :] for n in at]
        for u in range(16):
            ref[d, u : u + 1, :] = c16[u]
        for u in range(8):
            ref[d, 16 + u : 17 + u, :] = jnp.where(left, p16[u], p16[u + 8])
        ref[d, 24:25, :] = posmat[pl.ds(d, 1), :]

    loads[1].wait()
    pack(got, me)
    pl.semaphore_wait(pltpu.get_barrier_semaphore(), DEVS - 1)

    def copy(src, dst, send, recv, to):
        return pltpu.make_async_remote_copy(
            src_ref=src, dst_ref=dst, send_sem=send, recv_sem=recv, device_id=to, device_id_type=MESH
        )

    sent_rows = pl.ds(0, SENT)
    most = pl.ds(0, DEVS - 1)

    def send_out(n, carry, count=2):
        to = [peer(n * 2 - 1 + v) for v in range(count)]
        d = [v[0] * 16 + v[1] for v in to]
        for v in range(count):
            pack(packed, d[v])
        for v in range(count):
            copy(packed.at[d[v], sent_rows], got.at[me, sent_rows], so, ro, to[v]).start()
        return carry

    lax.fori_loop(1, DEVS // 2, send_out, 0)
    send_out(DEVS // 2, 0, 1)
    all_out = copy(packed.at[most, sent_rows], got.at[most, sent_rows], so, ro, peer(1))

    def zero(t, carry):
        ob[t] = jnp.zeros((LEAF, 128), F32)
        return carry

    lax.fori_loop(0, 32, zero, 0)
    all_out.wait_recv()

    arrived = jnp.transpose(got[:, 24, :])[0:16, :].astype(I32) & (ROWS - 1)
    pos_v[...] = arrived
    sub = lax.broadcasted_iota(I32, (128, 128), 0)
    lane = lax.broadcasted_iota(I32, (128, 128), 1).astype(F32)
    both = jnp.zeros((256, 16), F32)
    for u in range(16):
        p = arrived[u : u + 1, :]
        hit = (sub == (p >> 4)).astype(F32)
        low = (sub[0:16] == (p & 15)).astype(F32).astype(BF16)
        pieces = jnp.concatenate([(hit * lane).astype(BF16), (hit * float(u)).astype(BF16)], axis=0)
        both = both + dot(pieces, low, ((1,), (1,)))
    inv_v[...] = slots_first(16.0 * both[0:128] + both[128:256])
    moves = [to_scalars(5, pos_v, pos), to_scalars(6, inv_v, inv)]
    for one in moves:
        one.start()

    def unpack(d, carry):
        rows = got[d, 16:24, :]
        wide[pl.ds(pl.multiple_of(d * 16, 16), 8), :] = rows
        wide[pl.ds(pl.multiple_of(d * 16 + 8, 8), 8), :] = pltpu.roll(rows, DIM, axis=1)
        return carry

    lax.fori_loop(0, DEVS, unpack, 0)
    for one in moves:
        one.wait()

    def place(h, g):
        def some(b, carry):
            at = [inv[u, h * 64 + g * 16 + b] for u in range(16)]
            c16 = [got[n >> 4, pl.ds(n & 15, 1), :] for n in at]
            p16 = [wide[pl.ds(n, 1), :] for n in at]
            first = pl.multiple_of(b * 16, 16)
            for u in range(16):
                blk[h, g, pl.ds(first + u, 1), :] = c16[u]
                pts[pl.ds(h * 1024 + g * HALF + first + u, 1), :] = p16[u]
            return carry

        lax.fori_loop(0, 16, some, 0)
        xt = jnp.transpose(pts[h * 1024 + g * HALF : h * 1024 + (g + 1) * HALF, :])
        blk[h, g, HALF : HALF + 64, :] = xt[0:64, 0:128]
        blk[h, g, HALF + 64 : BLK, :] = xt[0:64, 128:256]

    def chain(h, k, leaf):
        (ax, az), (bx, bz) = CHAIN[k - 1], CHAIN[k]
        to = (o, from_me(h, (bx - ax, bz - az)))
        return copy(hub[h][k - 1].at[leaf], hub[h][k].at[leaf], sc.at[h, k - 1, leaf], rc.at[h, k - 1, leaf], to)

    def beside(h, n):
        return copy(sb.at[h, n], rb.at[h, n], ss.at[h, n], rs.at[h, n], (o, from_me(h, BESIDE[n][2])))

    def fbuf(dy, dc, lo=0, n=4):
        return fb.at[pl.ds((dy * 2 + dc - 1) * 4 + lo, n)]

    far_copies = {
        "up": copy(fblk, fbuf(1, 0), sf.at[0], rf.at[0], along_y(1)),
        "down": copy(fblk, fbuf(3, 0), sf.at[1], rf.at[1], along_y(-1)),
        "own": copy(fblk, fbuf(0, 1), sf.at[2], rf.at[2], sibling),
        "up2": copy(fbuf(1, 0, 0, 2), fbuf(2, 0, 0, 2), sf.at[3], rf.at[3], along_y(1)),
        "down2": copy(fbuf(3, 0, 2, 2), fbuf(2, 0, 2, 2), sf.at[4], rf.at[4], along_y(-1)),
        "side1": copy(fbuf(1, 0), fbuf(1, 1), sf.at[5], rf.at[5], sibling),
        "side3": copy(fbuf(3, 0), fbuf(3, 1), sf.at[6], rf.at[6], sibling),
        "side2": copy(fbuf(2, 0), fbuf(2, 1), sf.at[7], rf.at[7], sibling),
    }

    def wanted(dest, src, j):
        return code[src * 2 + j, (o * 16 + dest) * 4]

    def choose(n):
        offset, k, way = BESIDE[n]
        for h in range(2):
            src, dest = from_me(h, CHAIN[k], -1), from_me(h, way)
            for j in range(2):
                leaf = wanted(dest, src, j) & 3
                sb[h, n, j] = blk[h, leaf] if k == 0 else hub[h][k][leaf]
            beside(h, n).start()

    def serve(k, leaf):
        for h in range(2):
            chain(h, k, leaf).wait_recv()
            if k < 5:
                chain(h, k + 1, leaf).start()

    def add_tile(h, offset, j, load):
        src = from_me(h, offset, -1)
        v = wanted(i, src, j)
        at = (((SIGN[h] * offset[0]) % 4) * 4 + (SIGN[h] * offset[1]) % 4) * 2 + j
        ob[at] += tile(tgt[(v >> 2) & 3], source_operand(load(v & 3), (v >> 4).astype(F32)))

    def chain_tiles(k):
        for h in range(2):
            for j in range(2):
                add_tile(h, CHAIN[k], j, lambda leaf, h=h: hub[h][k][leaf])

    def beside_tiles(n):
        for h in range(2):
            beside(h, n).wait_recv()
            for j in range(2):
                add_tile(h, BESIDE[n][0], j, lambda leaf, h=h, j=j: rb[h, n, j])

    def halves(g):
        return [pl.ds(h * 1024 + g * HALF, HALF) for h in range(2)]

    def prepare(g):
        def pick(b, carry):
            at = [skel[g, b * 16 + u] for u in range(16)]
            rows = [pts[pl.ds((q >> 8) * 1024 + g * HALF + (q & 255), 1), :] for q in at]
            for u in range(16):
                sk[pl.ds(b * 16 + u, 1), :] = rows[u]
            return carry

        lax.fori_loop(0, 16, pick, 0)
        skt = jnp.transpose(sk[...])
        fblk[g, HALF : HALF + 64, :] = skt[0:64, 0:128]
        fblk[g, HALF + 64 : BLK, :] = skt[0:64, 128:256]
        stgt[g] = target_operand(sk[:, 0:DIM])
        charges = jnp.zeros((HALF, RHS), F32)
        for h, rows in enumerate(halves(g)):
            tgt[g, h * HALF : (h + 1) * HALF, :] = target_operand(pts[rows, 0:DIM])
            weights = interp[g * LEAF + h * HALF : g * LEAF + (h + 1) * HALF, :]
            charges = charges + dot3(weights, blk[h, g, 0:HALF, :], ((0,), (0,)))
        fblk[g, 0:HALF, :] = charges

    def own_tiles(g):
        near = tile(tgt[g], source_operand(blk[0, g], None)) + tile(tgt[g], source_operand(blk[1, g], None))
        for h, rows in enumerate(halves(g)):
            pot[rows, :] = near[h * HALF : (h + 1) * HALF, :]

    def far_leaf(g):
        def one(k, q):
            return q + tile(stgt[g], source_operand(fb[far_at[k, mine + g]], None))

        q = lax.fori_loop(0, 8, one, jnp.zeros((HALF, 128), F32))
        more = dot3(interp[g * LEAF : (g + 1) * LEAF, :], q)
        for h, rows in enumerate(halves(g)):
            pot[rows, :] += more[h * HALF : (h + 1) * HALF, :]

    for leaf in range(4):
        for h in range(2):
            place(h, leaf)
            chain(h, 1, leaf).start()
    choose(1)
    loads[2].wait()
    prepare(0)
    serve(1, 0)
    prepare(1)
    prepare(2)
    serve(1, 1)
    serve(2, 0)
    prepare(3)
    for name in ("up", "down", "own"):
        far_copies[name].start()
    serve(1, 2)
    serve(2, 1)
    own_tiles(0)
    own_tiles(1)
    serve(1, 3)
    serve(2, 2)
    choose(2)
    own_tiles(2)
    serve(2, 3)
    serve(3, 0)
    choose(3)
    own_tiles(3)
    serve(3, 1)
    serve(4, 0)
    chain_tiles(1)
    serve(3, 2)
    serve(4, 1)
    for name, more in (("up", ("up2", "side1")), ("down", ("down2", "side3")), ("own", ())):
        far_copies[name].wait_recv()
        for m in more:
            far_copies[m].start()
    chain_tiles(2)
    serve(3, 3)
    serve(4, 2)
    choose(4)
    beside_tiles(1)
    serve(4, 3)
    choose(0)
    serve(5, 0)
    choose(5)
    choose(6)
    for name in ("up2", "down2"):
        far_copies[name].wait_recv()
    far_copies["side2"].start()
    chain_tiles(3)
    serve(5, 1)
    chain_tiles(4)
    serve(5, 2)
    beside_tiles(2)
    serve(5, 3)
    for n in (7, 8, 9):
        choose(n)
    for name in ("side1", "side3", "side2"):
        far_copies[name].wait_recv()
    for g in range(4):
        far_leaf(g)
    chain_tiles(5)
    for n in (0, 3, 4, 6, 5, 8, 7, 9):
        beside_tiles(n)

    for g in range(4):
        at = [near_at[k, mine + g] for k in range(1, 8)]
        for h, rows in enumerate(halves(g)):
            total = pot[rows, :]
            for k in range(7):
                total = total + ob[at[k], h * HALF : (h + 1) * HALF, :]
            pot[rows, :] = total

    def gather(ref, at, d):
        rows = [pot[pl.ds(pos[u, d], 1), :] for u in range(16)]
        for u in range(16):
            ref[at, u : u + 1, :] = rows[u]

    def send_back(n, carry, count=2):
        to = [peer(n * 2 - 1 + v) for v in range(count)]
        d = [v[0] * 16 + v[1] for v in to]
        for v in range(count):
            gather(leaving, d[v], d[v])
        for v in range(count):
            copy(leaving.at[d[v]], landed.at[me], sl, rl, to[v]).start()
        return carry

    lax.fori_loop(1, DEVS // 2, send_back, 0)
    send_back(DEVS // 2, 0, 1)
    gather(landed, me, me)
    for h in range(2):
        for k in range(1, 6):
            for leaf in range(4):
                chain(h, k, leaf).wait_send()
        for n in range(10):
            beside(h, n).wait_send()
    for one in far_copies.values():
        one.wait_send()
    whole = copy(leaving.at[most], landed.at[most], sl, rl, peer(1))
    whole.wait_recv()

    def spread(b, carry):
        first = pl.multiple_of(b * 16, 16)
        at = [rank[b >> 3, (b & 7) * 16 + u] for u in range(16)]
        rows = [landed[n >> 4, pl.ds(n & 15, 1), :] for n in at]
        for u in range(16):
            out[pl.ds(first + u, 1), :] = rows[u]
        return carry

    saves = []
    for q in range(4):
        lax.fori_loop(q * (ROWS // 64), (q + 1) * (ROWS // 64), spread, 0)
        rows = pl.ds(q * (ROWS // 4), ROWS // 4)
        saves.append(pltpu.make_async_copy(out.at[rows], out_hbm.at[rows], sh.at[3 + q]))
        saves[-1].start()
    whole.wait_send()
    for one in saves:
        one.wait()
    all_out.wait_send()


def exchange(order, near, far, skel, points, charges, interp):
    dma = pltpu.SemaphoreType.DMA
    return pl.pallas_call(
        exchange_kernel,
        out_shape=jax.ShapeDtypeStruct((ROWS, RHS), F32),
        in_specs=[vspec()] * 3 + [sspec()] + [pl.BlockSpec(memory_space=pl.ANY)] * 3,
        out_specs=pl.BlockSpec(memory_space=pl.ANY),
        scratch_shapes=[
            pltpu.VMEM((DIM, ROWS), F32),
            pltpu.VMEM((ROWS, RHS), F32),
            pltpu.VMEM((ROWS, 256), F32),
            pltpu.VMEM((ROWS, RHS), F32),
            dma((7,)),
            pltpu.VMEM((16, 128), I32),
            pltpu.VMEM((16, 128), I32),
            pltpu.VMEM((DEVS, 128), F32),
            pltpu.VMEM((32, near.shape[0]), I32),
            pltpu.VMEM((8, near.shape[0]), I32),
            pltpu.VMEM((8, near.shape[0]), I32),
            pltpu.VMEM((16, 128), I32),
            pltpu.VMEM((16, 128), I32),
            pltpu.SMEM((16, 128), I32),
            pltpu.SMEM((16, 128), I32),
            pltpu.SMEM((32, near.shape[0]), I32),
            pltpu.SMEM((8, near.shape[0]), I32),
            pltpu.SMEM((8, near.shape[0]), I32),
            pltpu.SMEM((16, 128), I32),
            pltpu.SMEM((16, 128), I32),
            dma((7,)),
            pltpu.VMEM((ROWS, 128), F32),
            pltpu.VMEM((DEVS, 32, 128), F32),
            pltpu.VMEM((DEVS, 32, 128), F32),
            dma,
            dma,
            pltpu.VMEM((2, 4, BLK, 128), F32),
            pltpu.VMEM((ROWS, 128), F32),
            pltpu.VMEM((ROWS, RHS), F32),
            pltpu.VMEM((DEVS, 16, RHS), F32),
            pltpu.VMEM((DEVS, 16, RHS), F32),
            pltpu.VMEM((4, BLK, 128), F32),
            pltpu.VMEM((4, LEAF, 256), BF16),
            pltpu.VMEM((4, HALF, 256), BF16),
            pltpu.VMEM((HALF, 128), F32),
        ]
        + [pltpu.VMEM((4, BLK, 128), F32)] * 10
        + [
            pltpu.VMEM((2, 10, 2, BLK, 128), F32),
            pltpu.VMEM((2, 10, 2, BLK, 128), F32),
            pltpu.VMEM((28, BLK, 128), F32),
            pltpu.VMEM((32, LEAF, 128), F32),
            dma((2, 5, 4)),
            dma((2, 5, 4)),
            dma((2, 10)),
            dma((2, 10)),
            dma((8,)),
            dma((8,)),
            dma,
            dma,
        ],
        compiler_params=pltpu.CompilerParams(
            vmem_limit_bytes=VMEM_LIMIT, collective_id=0, has_side_effects=True
        ),
    )(order.reshape(16, 128), near.T, far.T, skel, points.T, charges, interp)


def shards(points, charges, interp, order, near, far, skel):
    return exchange(order, near, far, skel, points, charges, interp)


def solution(mesh):
    rows = P(("outer", "inner"), None)
    return jax.shard_map(
        shards,
        mesh=mesh,
        in_specs=(rows, rows, rows, P(("outer", "inner")), P(), P(), rows),
        out_specs=rows,
        check_vma=False,
    )
```
